256 devices in a mesh: row: 16 (over z, x_hi), col: 16 (over y, x_lo, core).
Axes of the slice: x: 4 (x_hi: 2, x_lo: 2; x = x_hi * 2 + x_lo), y: 4, z: 8, core: 2. Of those that a mesh axis runs over, the one named last changes fastest.
Arguments:
- snapshot: bfloat16 [1024, 1024, 512], P('row', 'col'), may hold values from -6 to 6
- basis_two: bfloat16 [1024, 128], P('col'), may hold values from -0.1875 to 0.1875
- basis_three: bfloat16 [512, 128], replicated, may hold values from -0.25 to 0.25
Outputs:
- gram: float32 [1024, 1024], P('row', 'col')
The draws below stay inside these ranges and needn't reach their ends.
All inputs are finite; a program needn't handle non-finite values.
Results may differ from the reference program's by a relative error of at most 0.0017.
Values may be sent and summed in bfloat16 or wider, within the bound.
A program may use at most 64 MiB of HBM per device.

```python
import jax
import jax.numpy as jnp
from jax import lax

I3 = 512
R2 = 128
R3 = 128
I1 = 1024
I2 = 1024


def levels(own_key, dims, cuts, smallest, top_value):
    level = 1.0
    for dim, blocks in cuts:
        steps = jax.random.uniform(jax.random.fold_in(jax.random.fold_in(own_key, 6), dim), (blocks,), jnp.float32, smallest / len(cuts), top_value / len(cuts))
        level = level * jnp.repeat(jnp.exp(steps), dims[dim] // blocks).reshape((-1,) + (1,) * (len(dims) - 1 - dim))
    return level


def normal_values(stream_key, dims, deviation, reach, split=(), held_as=jnp.bfloat16):
    result = jax.random.normal(stream_key, dims, jnp.float32) * deviation
    if len(split) > 0:
        result = levels(stream_key, dims, split, -0.22, 0.18) * result
    return jnp.clip(result, min=-reach, max=reach).astype(held_as)


def setup_inputs(seed: int = 0) -> dict:
    seeds = jax.random.split(jax.random.key(seed), 4)
    snapshot = normal_values(seeds[0], (I1, I2, I3), 1.0, 6.0, ((0, 16), (1, 16)))
    basis_two = normal_values(seeds[1], (I2, R2), I2 ** -0.5, 0.1875, ((0, 16),))
    basis_three = normal_values(seeds[2], (I3, R3), I3 ** -0.5, 0.25)
    return dict(snapshot=snapshot, basis_two=basis_two, basis_three=basis_three)


def reference(snapshot, basis_two, basis_three):
    block_rows = 8 if I1 % 8 == 0 else 1
    blocks = snapshot.reshape(I1 // block_rows, block_rows, I2, I3)
    second = basis_two.astype(jnp.float32)

    def project(block):
        inner = jnp.dot(block.reshape(block_rows * I2, I3), basis_three, preferred_element_type=jnp.float32)
        inner = lax.optimization_barrier(inner.astype(jnp.bfloat16)).astype(jnp.float32)
        inner = inner.reshape(block_rows, I2, R3)
        return jnp.einsum("abr,bq->aqr", inner, second, precision=lax.Precision.HIGHEST)

    projected = lax.map(project, blocks).reshape(I1, R2 * R3)
    rounded = projected.astype(jnp.bfloat16)
    total = jnp.dot(rounded, rounded.T, preferred_element_type=jnp.float32)
    return total * (1.0 / (R2 * R3))
```

```python
import jax
import jax.numpy as jnp
from jax import lax
from jax.experimental import pallas as pl
from jax.experimental.pallas import tpu as pltpu
from jax.sharding import PartitionSpec as P

MESH = pl.DeviceIdType.MESH
NT = (((1,), (1,)), ((), ()))

N_COL = 16
PLANES = 8
STAGES = 4
OFFSETS = (0, -2, -1, 2)
BLOCKS = ((0, 0), (0, 2), (2, 0), (0, 3), (3, 0), (2, 3), (3, 2), (1, 3))


def kernel(
    snap_hbm,
    b2_ref,
    b3_ref,
    out_ref,
    snap,
    b3t,
    factor,
    weights,
    outgoing,
    incoming,
    pacc,
    half_out,
    rows,
    grams,
    parts,
    load_sems,
    factor_sems,
    a_send,
    a_recv,
    x_send,
    x_recv,
    z_send,
    z_recv,
    g_send,
    g_recv,
):
    row = lax.axis_index("row")
    col = lax.axis_index("col")
    z = row // 2
    xh = lax.rem(row, 2)
    core = lax.rem(col, 2)

    def plane(offset):
        return lax.rem(z + offset + PLANES, PLANES)

    loads = [
        pltpu.make_async_copy(snap_hbm.at[pl.ds(16 * s, 16)], snap.at[s], load_sems.at[s])
        for s in range(STAGES)
    ]
    for load in loads:
        load.start()

    barrier = pltpu.get_barrier_semaphore()

    def greet(i, carry):
        peer = lax.rem(col + i, N_COL)
        pl.semaphore_signal(barrier, inc=1, device_id=(row, peer), device_id_type=MESH)
        return carry

    lax.fori_loop(1, N_COL, greet, 0)
    pl.semaphore_signal(barrier, inc=1, device_id=(z * 2 + 1 - xh, col), device_id_type=MESH)
    for offset in OFFSETS[1:]:
        pl.semaphore_signal(barrier, inc=1, device_id=(plane(offset) * 2 + xh, col), device_id_type=MESH)

    b3t[...] = b3_ref[...].T

    def first_product(s):
        loads[s].wait()
        left = b3t[...]
        for jp in range(4):
            right = jnp.concatenate(
                [snap[s, 2 * jp], snap[s, 8 + 2 * jp], snap[s, 2 * jp + 1], snap[s, 9 + 2 * jp]], axis=0
            )
            inner = lax.dot_general(left, right, NT, preferred_element_type=jnp.float32)
            pair = jnp.concatenate(
                [inner[:, :128].reshape(N_COL, 8, 128), inner[:, 128:].reshape(N_COL, 8, 128)], axis=1
            ).astype(jnp.bfloat16)
            outgoing[s, :, jp] = pair
        incoming[s, col] = outgoing[s, col]

    def send_stage(s):
        def body(i, carry):
            peer = col ^ i
            pltpu.make_async_remote_copy(
                src_ref=outgoing.at[s, peer],
                dst_ref=incoming.at[s, col],
                send_sem=a_send.at[s],
                recv_sem=a_recv.at[s],
                device_id=(row, peer),
                device_id_type=MESH,
            ).start()
            return carry

        lax.fori_loop(1, N_COL, body, 0)

    def stage_copy(s):
        return pltpu.make_async_remote_copy(
            src_ref=outgoing.at[s, pl.ds(0, N_COL - 1)],
            dst_ref=incoming.at[s, pl.ds(0, N_COL - 1)],
            send_sem=a_send.at[s],
            recv_sem=a_recv.at[s],
            device_id=(row, col),
            device_id_type=MESH,
        )

    first_product(0)
    pl.semaphore_wait(barrier, N_COL - 1 + 1 + 3)

    def send_factor(i, carry):
        peer = col ^ i
        pltpu.make_async_remote_copy(
            src_ref=b2_ref,
            dst_ref=factor.at[col],
            send_sem=factor_sems.at[0],
            recv_sem=factor_sems.at[1],
            device_id=(row, peer),
            device_id_type=MESH,
        ).start()
        return carry

    lax.fori_loop(1, N_COL, send_factor, 0)
    send_stage(0)
    factor[col] = b2_ref[...]
    for s in range(1, STAGES):
        first_product(s)
        send_stage(s)

    factor_copy = pltpu.make_async_remote_copy(
        src_ref=factor.at[pl.ds(0, N_COL - 1)],
        dst_ref=factor.at[pl.ds(0, N_COL - 1)],
        send_sem=factor_sems.at[0],
        recv_sem=factor_sems.at[1],
        device_id=(row, col),
        device_id_type=MESH,
    )
    factor_copy.wait_recv()
    weights[...] = jnp.zeros_like(weights)
    for c in range(N_COL):
        block = factor[c]
        weights[pl.ds(c * 128, 64), :128] = block
        weights[pl.ds(c * 128 + 64, 64), 128:] = block

    def x_copy(s):
        return pltpu.make_async_remote_copy(
            src_ref=half_out.at[s],
            dst_ref=rows.at[0, xh, s],
            send_sem=x_send.at[s],
            recv_sem=x_recv.at[s],
            device_id=(z * 2 + 1 - xh, col),
            device_id_type=MESH,
        )

    def send_rows(s, side):
        for slot in range(1, len(OFFSETS)):
            pltpu.make_async_remote_copy(
                src_ref=rows.at[0, side, s],
                dst_ref=rows.at[slot, side, s],
                send_sem=z_send,
                recv_sem=z_recv,
                device_id=(plane(-OFFSETS[slot]) * 2 + xh, col),
                device_id_type=MESH,
            ).start()

    def second_product(s):
        stage_copy(s).wait_recv()
        total = jnp.zeros((64, 256), jnp.float32)
        for c in range(0, N_COL, 2):
            left = jnp.concatenate(
                [incoming[s, c].reshape(64, 128), incoming[s, c + 1].reshape(64, 128)], axis=1
            )
            total = total + jnp.dot(left, weights[pl.ds(c * 128, 256), :], preferred_element_type=jnp.float32)
        pacc[0] = total[:, :128]
        pacc[1] = total[:, 128:]
        for r in range(4):
            halves = []
            for h in range(2):
                every = pl.ds(4 * h + r, 8, stride=8)
                halves.append(jnp.concatenate([pacc[0, every, :], pacc[1, every, :]], axis=0))
            lanes = pl.ds(r * 128, 128)
            rows[0, xh, s, :, lanes] = jnp.where(xh == 0, halves[0], halves[1]).astype(jnp.bfloat16)
            half_out[s, :, lanes] = jnp.where(xh == 0, halves[1], halves[0]).astype(jnp.bfloat16)

    for s in range(STAGES):
        second_product(s)
        x_copy(s).start()
        send_rows(s, xh)
        if s > 0:
            x_copy(s - 1).wait_recv()
            send_rows(s - 1, 1 - xh)
    x_copy(STAGES - 1).wait_recv()
    send_rows(STAGES - 1, 1 - xh)

    z_copy = pltpu.make_async_remote_copy(
        src_ref=rows.at[pl.ds(1, 3)],
        dst_ref=rows.at[pl.ds(1, 3)],
        send_sem=z_send,
        recv_sem=z_recv,
        device_id=(row, col),
        device_id_type=MESH,
    )
    z_copy.wait_recv()

    me = xh * N_COL + col
    low = lax.broadcasted_iota(jnp.int32, (64, 128), 1) < 64

    def gram_target(b, i):
        slot_u, slot_v = BLOCKS[b]
        to_row = plane(OFFSETS[slot_u]) * 2 + i // 2
        to_col = plane(OFFSETS[slot_v]) * 2 + lax.rem(i, 2)
        return to_row, to_col

    for b, (slot_u, slot_v) in enumerate(BLOCKS):
        upper = rows[slot_u, :, 0:2].reshape(64, 512)
        lower = rows[slot_u, :, 2:4].reshape(64, 512)
        right = rows[slot_v].reshape(128, 512)
        swapped = jnp.concatenate([rows[slot_v, 1].reshape(64, 512), rows[slot_v, 0].reshape(64, 512)], axis=0)
        m1 = lax.dot_general(upper, right, NT, preferred_element_type=jnp.float32)
        m2 = lax.dot_general(lower, swapped, NT, preferred_element_type=jnp.float32)
        for_core0 = jnp.where(low, m1, m2).reshape(2, 32, 128)
        for_core1 = jnp.where(low, m2, m1).reshape(2, 32, 128)
        for xu in range(2):
            grams[b, 2 * xu] = for_core0[xu]
            grams[b, 2 * xu + 1] = for_core1[xu]

        def send_gram(i, carry):
            to_row, to_col = gram_target(b, i)
            own = jnp.logical_and(to_row == row, to_col == col)

            @pl.when(own)
            def _():
                pltpu.make_async_copy(grams.at[b, i], parts.at[me], g_recv).start()

            @pl.when(jnp.logical_not(own))
            def _():
                pltpu.make_async_remote_copy(
                    src_ref=grams.at[b, i],
                    dst_ref=parts.at[me],
                    send_sem=g_send.at[b],
                    recv_sem=g_recv,
                    device_id=(to_row, to_col),
                    device_id_type=MESH,
                ).start()

            return carry

        lax.fori_loop(0, 4, send_gram, 0)

    pltpu.make_async_copy(parts, parts, g_recv).wait()
    total = jnp.sum(parts[...], axis=0) * (1.0 / 16384.0)
    first, second = total[:, :64], total[:, 64:]
    out_ref[0:32, :] = jnp.where(core == 0, first, second)
    out_ref[32:64, :] = jnp.where(core == 0, second, first)

    factor_copy.wait_send()
    for s in range(STAGES):
        stage_copy(s).wait_send()
        x_copy(s).wait_send()
    z_copy.wait_send()
    for b in range(len(BLOCKS)):

        def end_gram(i, carry):
            to_row, to_col = gram_target(b, i)

            @pl.when(jnp.logical_not(jnp.logical_and(to_row == row, to_col == col)))
            def _():
                pltpu.make_async_remote_copy(
                    src_ref=grams.at[b, i],
                    dst_ref=parts.at[me],
                    send_sem=g_send.at[b],
                    recv_sem=g_recv,
                    device_id=(to_row, to_col),
                    device_id_type=MESH,
                ).wait_send()

            return carry

        lax.fori_loop(0, 4, end_gram, 0)


def on_device(snapshot, basis_two, basis_three):
    vmem = pl.BlockSpec(memory_space=pltpu.VMEM)
    bf16, f32 = jnp.bfloat16, jnp.float32
    dma = pltpu.SemaphoreType.DMA
    return pl.pallas_call(
        kernel,
        out_shape=jax.ShapeDtypeStruct((64, 64), f32),
        in_specs=[pl.BlockSpec(memory_space=pltpu.HBM), vmem, vmem],
        out_specs=vmem,
        scratch_shapes=[
            pltpu.VMEM((STAGES, 16, 64, 512), bf16),
            pltpu.VMEM((128, 512), bf16),
            pltpu.VMEM((N_COL, 64, 128), bf16),
            pltpu.VMEM((N_COL * 128, 256), bf16),
            pltpu.VMEM((STAGES, N_COL, 4, 16, 128), bf16),
            pltpu.VMEM((STAGES, N_COL, 4, 16, 128), bf16),
            pltpu.VMEM((2, 64, 128), f32),
            pltpu.VMEM((STAGES, 16, 512), bf16),
            pltpu.VMEM((4, 2, STAGES, 16, 512), bf16),
            pltpu.VMEM((len(BLOCKS), 4, 32, 128), f32),
            pltpu.VMEM((2 * N_COL, 32, 128), f32),
            dma((STAGES,)),
            dma((2,)),
            dma((STAGES,)),
            dma((STAGES,)),
            dma((STAGES,)),
            dma((STAGES,)),
            dma,
            dma,
            dma((len(BLOCKS),)),
            dma,
        ],
        compiler_params=pltpu.CompilerParams(
            collective_id=0, has_side_effects=True, vmem_limit_bytes=48 * 1024 * 1024
        ),
    )(snapshot, basis_two, basis_three)


def solution(mesh):
    in_specs = (P("row", "col", None), P("col", None), P())
    return jax.shard_map(
        on_device, mesh=mesh, in_specs=in_specs, out_specs=P("row", "col"), check_vma=False
    )
```

```python
import jax
import jax.numpy as jnp
from jax import lax
from jax.experimental import pallas as pl
from jax.experimental.pallas import tpu as pltpu
from jax.sharding import PartitionSpec as P

MESH = pl.DeviceIdType.MESH
NT = (((1,), (1,)), ((), ()))

N_COL = 16
PLANES = 8
STAGES = 4
OFFSETS = (0, -2, -1, 2)
BLOCKS = ((3, 0), (3, 2), (1, 3), (2, 0), (2, 3), (0, 3), (0, 2), (0, 0))


def kernel(
    snap_hbm,
    b2_hbm,
    b3_hbm,
    out_ref,
    snap,
    b3,
    b3t,
    factor,
    weights,
    outgoing,
    incoming,
    pacc,
    half_out,
    rows,
    grams,
    mates,
    sums,
    parts,
    load_sems,
    f_sems,
    a_send,
    a_recv,
    z_send,
    z_recv,
    m_send,
    m_recv,
    g_send,
    g_recv,
):
    row = lax.axis_index("row")
    col = lax.axis_index("col")
    z = row // 2
    xh = lax.rem(row, 2)
    core = lax.rem(col, 2)
    chip = col // 2
    across = (1 - xh, col ^ 2)

    def plane(offset):
        return lax.rem(z + offset + PLANES, PLANES)

    def remote(src, dst, send_sem, recv_sem, device):
        return pltpu.make_async_remote_copy(
            src_ref=src,
            dst_ref=dst,
            send_sem=send_sem,
            recv_sem=recv_sem,
            device_id=device,
            device_id_type=MESH,
        )

    here = (row, col)
    load_b3 = pltpu.make_async_copy(b3_hbm, b3, load_sems.at[STAGES])
    load_b2 = pltpu.make_async_copy(b2_hbm, factor.at[core, chip], load_sems.at[STAGES + 1])
    loads = [
        pltpu.make_async_copy(snap_hbm.at[pl.ds(16 * s, 16)], snap.at[s], load_sems.at[s])
        for s in range(STAGES)
    ]
    load_b3.start()
    loads[0].start()
    load_b2.start()
    for load in loads[1:]:
        load.start()

    barrier = pltpu.get_barrier_semaphore()

    def greet(device):
        pl.semaphore_signal(barrier, inc=1, device_id=device, device_id_type=MESH)

    def greet_column(i, carry):
        greet((row, col ^ i))
        return carry

    lax.fori_loop(1, N_COL, greet_column, 0)
    for offset in OFFSETS[1:]:
        greet((plane(offset) * 2 + xh, col))
    for offset in OFFSETS:
        greet((plane(offset) * 2 + across[0], across[1]))
    for y in range(1, 4):
        greet((z * 2 + across[0], across[1] ^ (4 * y)))

    load_b3.wait()
    b3t[...] = b3[...].T

    def first_product(s):
        loads[s].wait()
        left = b3t[...]
        for jp in range(4):
            right = jnp.concatenate(
                [snap[s, 2 * jp], snap[s, 8 + 2 * jp], snap[s, 2 * jp + 1], snap[s, 9 + 2 * jp]], axis=0
            )
            inner = lax.dot_general(left, right, NT, preferred_element_type=jnp.float32)
            pair = jnp.concatenate(
                [inner[:, :128].reshape(N_COL, 8, 128), inner[:, 128:].reshape(N_COL, 8, 128)], axis=1
            ).astype(jnp.bfloat16)
            outgoing[s, :, jp] = pair
        incoming[s, col] = outgoing[s, col ^ (2 * xh)]

    def send_stage(s):
        def body(i, carry):
            peer = col ^ i
            remote(
                outgoing.at[s, peer ^ (2 * xh)], incoming.at[s, col], a_send.at[s], a_recv.at[s], (row, peer)
            ).start()
            return carry

        lax.fori_loop(1, N_COL, body, 0)

    def stage_copy(s):
        most = pl.ds(0, N_COL - 1)
        return remote(outgoing.at[s, most], incoming.at[s, most], a_send.at[s], a_recv.at[s], here)

    first_product(0)
    load_b2.wait()
    pl.semaphore_wait(barrier, N_COL - 1 + 3 + 4 + 3)

    send_stage(0)
    own = factor.at[core, chip]
    for y in range(1, 4):
        remote(own, own, f_sems.at[0], f_sems.at[1], (row, col ^ (4 * y))).start()
    for y in range(4):
        remote(own, own, f_sems.at[0], f_sems.at[1], (z * 2 + across[0], across[1] ^ (4 * y))).start()
    for s in range(1, STAGES):
        first_product(s)
        send_stage(s)

    most = factor.at[core, pl.ds(0, 7)]
    factor_copy = remote(most, most, f_sems.at[0], f_sems.at[1], here)
    factor_copy.wait_recv()
    mate = (row, col ^ 1)
    mine = factor.at[core]
    mate_copy = remote(mine, mine, f_sems.at[2], f_sems.at[3], mate)
    mate_copy.start()
    weights[...] = jnp.zeros_like(weights)
    mate_copy.wait_recv()
    for c in range(N_COL):
        block = factor[c % 2, c // 2]
        weights[pl.ds(c * 128, 64), :128] = block
        weights[pl.ds(c * 128 + 64, 64), 128:] = block

    def send_rows(s):
        for slot, offset in enumerate(OFFSETS):
            to = plane(-offset) * 2
            if slot:
                remote(rows.at[0, xh, s], rows.at[slot, xh, s], z_send.at[0], z_recv.at[0], (to + xh, col)).start()
            which = 0 if slot else 1
            remote(
                half_out.at[s],
                rows.at[slot, xh, s],
                z_send.at[which],
                z_recv.at[which],
                (to + across[0], across[1]),
            ).start()

    def second_product(s):
        stage_copy(s).wait_recv()
        total = jnp.zeros((64, 256), jnp.float32)
        for c in range(0, N_COL, 2):
            left = jnp.concatenate(
                [incoming[s, c].reshape(64, 128), incoming[s, c + 1].reshape(64, 128)], axis=1
            )
            total = total + jnp.dot(left, weights[pl.ds(c * 128, 256), :], preferred_element_type=jnp.float32)
        pacc[0] = total[:, :128]
        pacc[1] = total[:, 128:]
        for r in range(4):
            halves = []
            for h in range(2):
                every = pl.ds(4 * h + r, 8, stride=8)
                halves.append(jnp.concatenate([pacc[0, every, :], pacc[1, every, :]], axis=0))
            lanes = pl.ds(r * 128, 128)
            rows[0, xh, s, :, lanes] = jnp.where(xh == 0, halves[0], halves[1]).astype(jnp.bfloat16)
            half_out[s, :, lanes] = jnp.where(xh == 0, halves[1], halves[0]).astype(jnp.bfloat16)

    for s in range(STAGES):
        second_product(s)
        send_rows(s)

    far = rows.at[pl.ds(1, 3)]
    near = rows.at[0, 0]
    far_copy = remote(far, far, z_send.at[0], z_recv.at[0], here)
    near_copy = remote(near, near, z_send.at[1], z_recv.at[1], here)
    near_copy.wait_recv()
    far_copy.wait_recv()

    low = lax.broadcasted_iota(jnp.int32, (64, 128), 1) < 64
    sender = xh * 8 + chip

    def mate_gram(b):
        return remote(grams.at[b, 1 - core], mates.at[b], m_send.at[b], m_recv.at[b], mate)

    def gram_copy(b, j):
        slot_u, slot_v = BLOCKS[b]
        to = (plane(OFFSETS[slot_u]) * 2 + core, plane(OFFSETS[slot_v]) * 2 + j)
        own = jnp.logical_and(to[0] == row, to[1] == col)
        return own, remote(sums.at[b, j], parts.at[sender], g_send.at[b], g_recv, to)

    def send_gram(b):
        mate_gram(b).wait_recv()
        sums[b] = grams[b, core] + mates[b]
        for j in range(2):
            own, copy = gram_copy(b, j)

            @pl.when(own)
            def _():
                pltpu.make_async_copy(sums.at[b, j], parts.at[sender], g_recv).start()

            @pl.when(jnp.logical_not(own))
            def _():
                copy.start()

    for b, (slot_u, slot_v) in enumerate(BLOCKS):
        upper = rows[slot_u, :, 0:2].reshape(64, 512)
        lower = rows[slot_u, :, 2:4].reshape(64, 512)
        right = rows[slot_v].reshape(128, 512)
        swapped = jnp.concatenate([rows[slot_v, 1].reshape(64, 512), rows[slot_v, 0].reshape(64, 512)], axis=0)
        m1 = lax.dot_general(upper, right, NT, preferred_element_type=jnp.float32)
        m2 = lax.dot_general(lower, swapped, NT, preferred_element_type=jnp.float32)
        grams[b, :, 0] = jnp.where(low, m1, m2).reshape(2, 32, 128)
        grams[b, :, 1] = jnp.where(low, m2, m1).reshape(2, 32, 128)
        mate_gram(b).start()
        if b:
            send_gram(b - 1)
    send_gram(len(BLOCKS) - 1)

    pltpu.make_async_copy(parts, parts, g_recv).wait()
    total = jnp.sum(parts[...], axis=0) * (1.0 / 16384.0)
    first, second = total[:, :64], total[:, 64:]
    out_ref[0:32, :] = jnp.where(core == 0, first, second)
    out_ref[32:64, :] = jnp.where(core == 0, second, first)

    factor_copy.wait_send()
    mate_copy.wait_send()
    for s in range(STAGES):
        stage_copy(s).wait_send()
    far_copy.wait_send()
    near_copy.wait_send()
    for b in range(len(BLOCKS)):
        mate_gram(b).wait_send()
        for j in range(2):
            own, copy = gram_copy(b, j)

            @pl.when(jnp.logical_not(own))
            def _():
                copy.wait_send()


def on_device(snapshot, basis_two, basis_three):
    anywhere = pl.BlockSpec(memory_space=pl.ANY)
    bf16, f32 = jnp.bfloat16, jnp.float32
    dma = pltpu.SemaphoreType.DMA
    n_blocks = len(BLOCKS)
    return pl.pallas_call(
        kernel,
        out_shape=jax.ShapeDtypeStruct((64, 64), f32),
        in_specs=[anywhere] * 3,
        out_specs=pl.BlockSpec(memory_space=pltpu.VMEM),
        scratch_shapes=[
            pltpu.VMEM((STAGES, 16, 64, 512), bf16),
            pltpu.VMEM((512, 128), bf16),
            pltpu.VMEM((128, 512), bf16),
            pltpu.VMEM((2, 8, 64, 128), bf16),
            pltpu.VMEM((N_COL * 128, 256), bf16),
            pltpu.VMEM((STAGES, N_COL, 4, 16, 128), bf16),
            pltpu.VMEM((STAGES, N_COL, 4, 16, 128), bf16),
            pltpu.VMEM((2, 64, 128), f32),
            pltpu.VMEM((STAGES, 16, 512), bf16),
            pltpu.VMEM((4, 2, STAGES, 16, 512), bf16),
            pltpu.VMEM((n_blocks, 2, 2, 32, 128), f32),
            pltpu.VMEM((n_blocks, 2, 32, 128), f32),
            pltpu.VMEM((n_blocks, 2, 32, 128), f32),
            pltpu.VMEM((N_COL, 32, 128), f32),
            dma((STAGES + 2,)),
            dma((4,)),
            dma((STAGES,)),
            dma((STAGES,)),
            dma((2,)),
            dma((2,)),
            dma((n_blocks,)),
            dma((n_blocks,)),
            dma((n_blocks,)),
            dma,
        ],
        compiler_params=pltpu.CompilerParams(
            collective_id=0, has_side_effects=True, vmem_limit_bytes=60 * 1024 * 1024
        ),
    )(snapshot, basis_two, basis_three)


def solution(mesh):
    in_specs = (P("row", "col", None), P("col", None), P())
    return jax.shard_map(
        on_device, mesh=mesh, in_specs=in_specs, out_specs=P("row", "col"), check_vma=False
    )
```

```python
import jax
import jax.numpy as jnp
from jax import lax
from jax.experimental import pallas as pl
from jax.experimental.pallas import tpu as pltpu
from jax.sharding import PartitionSpec as P

MESH = pl.DeviceIdType.MESH
NT = (((1,), (1,)), ((), ()))

N_COL = 16
PLANES = 8
STAGES = 8
LAG = 3
ROWS = 64 // STAGES
HALF = ROWS // 2
PAIRS = HALF // 2
OFFSETS = (0, -2, -1, 2)
BLOCKS = ((0, 0), (2, 0), (0, 2), (3, 0), (0, 3), (3, 2), (2, 3), (1, 3))


def kernel(
    snap_hbm,
    b2_hbm,
    b3_hbm,
    out_ref,
    snap,
    b3,
    b3t,
    factor,
    weights,
    outgoing,
    incoming,
    pacc,
    half_out,
    rows,
    grams,
    mates,
    sums,
    parts,
    load_sems,
    f_sems,
    a_send,
    a_recv,
    z_send,
    z_recv,
    m_send,
    m_recv,
    g_send,
    g_recv,
):
    row = lax.axis_index("row")
    col = lax.axis_index("col")
    z = row // 2
    xh = lax.rem(row, 2)
    core = lax.rem(col, 2)
    chip = col // 2
    across = (1 - xh, col ^ 2)

    def plane(offset):
        return lax.rem(z + offset + PLANES, PLANES)

    def remote(src, dst, send_sem, recv_sem, device):
        return pltpu.make_async_remote_copy(
            src_ref=src,
            dst_ref=dst,
            send_sem=send_sem,
            recv_sem=recv_sem,
            device_id=device,
            device_id_type=MESH,
        )

    here = (row, col)
    load_b3 = pltpu.make_async_copy(b3_hbm, b3, load_sems.at[STAGES])
    load_b2 = pltpu.make_async_copy(b2_hbm, factor.at[core, chip], load_sems.at[STAGES + 1])
    loads = [
        pltpu.make_async_copy(snap_hbm.at[pl.ds(ROWS * s, ROWS)], snap.at[s], load_sems.at[s])
        for s in range(STAGES)
    ]
    load_b3.start()
    loads[0].start()
    load_b2.start()
    for load in loads[1:]:
        load.start()

    barrier = pltpu.get_barrier_semaphore()

    def greet(device):
        pl.semaphore_signal(barrier, inc=1, device_id=device, device_id_type=MESH)

    def greet_column(i, carry):
        greet((row, col ^ i))
        return carry

    lax.fori_loop(1, N_COL, greet_column, 0)
    for offset in OFFSETS[1:]:
        greet((plane(offset) * 2 + xh, col))
    for offset in OFFSETS:
        greet((plane(offset) * 2 + across[0], across[1]))
    for y in range(1, 4):
        greet((z * 2 + across[0], across[1] ^ (4 * y)))

    load_b3.wait()
    b3t[...] = b3[...].T

    def first_product(s):
        loads[s].wait()
        left = b3t[...]
        for jp in range(PAIRS):
            j = 2 * jp
            right = jnp.concatenate(
                [snap[s, j], snap[s, HALF + j], snap[s, j + 1], snap[s, HALF + j + 1]], axis=0
            )
            inner = lax.dot_general(left, right, NT, preferred_element_type=jnp.float32)
            pair = jnp.concatenate(
                [inner[:, :128].reshape(N_COL, 8, 128), inner[:, 128:].reshape(N_COL, 8, 128)], axis=1
            ).astype(jnp.bfloat16)
            outgoing[s, :, jp] = pair
        incoming[s, col] = outgoing[s, col ^ (2 * xh)]

    def send_stage(s):
        def body(i, carry):
            peer = col ^ i
            remote(
                outgoing.at[s, peer ^ (2 * xh)], incoming.at[s, col], a_send.at[s], a_recv.at[s], (row, peer)
            ).start()
            return carry

        lax.fori_loop(1, N_COL, body, 0)

    def stage_copy(s):
        most = pl.ds(0, N_COL - 1)
        return remote(outgoing.at[s, most], incoming.at[s, most], a_send.at[s], a_recv.at[s], here)

    first_product(0)
    load_b2.wait()
    pl.semaphore_wait(barrier, N_COL - 1 + 3 + 4 + 3)

    own = factor.at[core, chip]
    for y in range(1, 4):
        remote(own, own, f_sems.at[0], f_sems.at[1], (row, col ^ (4 * y))).start()
    for y in range(4):
        remote(own, own, f_sems.at[0], f_sems.at[1], (z * 2 + across[0], across[1] ^ (4 * y))).start()
    send_stage(0)
    for s in range(1, STAGES):
        first_product(s)
        send_stage(s)

    most = factor.at[core, pl.ds(0, 7)]
    factor_copy = remote(most, most, f_sems.at[0], f_sems.at[1], here)
    factor_copy.wait_recv()
    mate = (row, col ^ 1)
    mine = factor.at[core]
    mate_copy = remote(mine, mine, f_sems.at[2], f_sems.at[3], mate)
    mate_copy.start()
    weights[...] = jnp.zeros_like(weights)
    mate_copy.wait_recv()
    for c in range(N_COL):
        block = factor[c % 2, c // 2]
        weights[pl.ds(c * 128, 64), :128] = block
        weights[pl.ds(c * 128 + 64, 64), 128:] = block

    def send_rows(s):
        for slot, offset in enumerate(OFFSETS):
            to = plane(-offset) * 2
            if slot:
                remote(rows.at[0, xh, s], rows.at[slot, xh, s], z_send.at[slot], z_recv.at[slot], (to + xh, col)).start()
            remote(
                half_out.at[s],
                rows.at[slot, xh, s],
                z_send.at[slot],
                z_recv.at[slot],
                (to + across[0], across[1]),
            ).start()

    def second_product(s):
        stage_copy(s).wait_recv()
        total = jnp.zeros((8 * HALF, 256), jnp.float32)
        for c in range(0, N_COL, 2):
            left = jnp.concatenate(
                [incoming[s, c].reshape(8 * HALF, 128), incoming[s, c + 1].reshape(8 * HALF, 128)], axis=1
            )
            total = total + jnp.dot(left, weights[pl.ds(c * 128, 256), :], preferred_element_type=jnp.float32)
        pacc[0] = total[:, :128]
        pacc[1] = total[:, 128:]
        for r in range(4):
            halves = []
            for h in range(2):
                every = pl.ds(4 * h + r, HALF, stride=8)
                halves.append(jnp.concatenate([pacc[0, every, :], pacc[1, every, :]], axis=0))
            lanes = pl.ds(r * 128, 128)
            rows[0, xh, s, :, lanes] = jnp.where(xh == 0, halves[0], halves[1]).astype(jnp.bfloat16)
            half_out[s, :, lanes] = jnp.where(xh == 0, halves[1], halves[0]).astype(jnp.bfloat16)

    for s in range(STAGES):
        second_product(s)
        send_rows(s)

    def slot_copy(slot):
        piece = rows.at[slot] if slot else rows.at[0, 0]
        return remote(piece, piece, z_send.at[slot], z_recv.at[slot], here)

    low = lax.broadcasted_iota(jnp.int32, (64, 128), 1) < 64
    sender = xh * 8 + chip

    def mate_gram(b):
        return remote(grams.at[b, 1 - core], mates.at[b], m_send.at[b], m_recv.at[b], mate)

    def gram_copy(b, j):
        slot_u, slot_v = BLOCKS[b]
        to = (plane(OFFSETS[slot_u]) * 2 + core, plane(OFFSETS[slot_v]) * 2 + j)
        own = jnp.logical_and(to[0] == row, to[1] == col)
        return own, remote(sums.at[b, j], parts.at[sender], g_send.at[b], g_recv, to)

    def send_gram(b):
        mate_gram(b).wait_recv()
        sums[b] = grams[b, core] + mates[b]
        for j in range(2):
            own, copy = gram_copy(b, j)

            @pl.when(own)
            def _():
                pltpu.make_async_copy(sums.at[b, j], parts.at[sender], g_recv).start()

            @pl.when(jnp.logical_not(own))
            def _():
                copy.start()

    arrived = set()
    for b, (slot_u, slot_v) in enumerate(BLOCKS):
        for slot in (slot_u, slot_v):
            if slot not in arrived:
                slot_copy(slot).wait_recv()
                arrived.add(slot)
        upper = rows[slot_u, :, : STAGES // 2].reshape(64, 512)
        lower = rows[slot_u, :, STAGES // 2 :].reshape(64, 512)
        right = rows[slot_v].reshape(128, 512)
        swapped = jnp.concatenate([rows[slot_v, 1].reshape(64, 512), rows[slot_v, 0].reshape(64, 512)], axis=0)
        m1 = lax.dot_general(upper, right, NT, preferred_element_type=jnp.float32)
        m2 = lax.dot_general(lower, swapped, NT, preferred_element_type=jnp.float32)
        grams[b, :, 0] = jnp.where(low, m1, m2).reshape(2, 32, 128)
        grams[b, :, 1] = jnp.where(low, m2, m1).reshape(2, 32, 128)
        mate_gram(b).start()
        if b >= LAG:
            send_gram(b - LAG)
    for b in range(len(BLOCKS) - LAG, len(BLOCKS)):
        send_gram(b)

    pltpu.make_async_copy(parts, parts, g_recv).wait()
    total = jnp.sum(parts[...], axis=0) * (1.0 / 16384.0)
    first, second = total[:, :64], total[:, 64:]
    out_ref[0:32, :] = jnp.where(core == 0, first, second)
    out_ref[32:64, :] = jnp.where(core == 0, second, first)

    factor_copy.wait_send()
    mate_copy.wait_send()
    for s in range(STAGES):
        stage_copy(s).wait_send()
    for slot in range(len(OFFSETS)):
        slot_copy(slot).wait_send()
    for b in range(len(BLOCKS)):
        mate_gram(b).wait_send()
        for j in range(2):
            own, copy = gram_copy(b, j)

            @pl.when(jnp.logical_not(own))
            def _():
                copy.wait_send()


def on_device(snapshot, basis_two, basis_three):
    anywhere = pl.BlockSpec(memory_space=pl.ANY)
    bf16, f32 = jnp.bfloat16, jnp.float32
    dma = pltpu.SemaphoreType.DMA
    n_blocks = len(BLOCKS)
    return pl.pallas_call(
        kernel,
        out_shape=pltpu.VMEM((64, 64), f32),
        in_specs=[anywhere] * 3,
        out_specs=pl.BlockSpec(memory_space=pltpu.VMEM),
        scratch_shapes=[
            pltpu.VMEM((STAGES, ROWS, 64, 512), bf16),
            pltpu.VMEM((512, 128), bf16),
            pltpu.VMEM((128, 512), bf16),
            pltpu.VMEM((2, 8, 64, 128), bf16),
            pltpu.VMEM((N_COL * 128, 256), bf16),
            pltpu.VMEM((STAGES, N_COL, PAIRS, 16, 128), bf16),
            pltpu.VMEM((STAGES, N_COL, PAIRS, 16, 128), bf16),
            pltpu.VMEM((2, 8 * HALF, 128), f32),
            pltpu.VMEM((STAGES, ROWS, 512), bf16),
            pltpu.VMEM((4, 2, STAGES, ROWS, 512), bf16),
            pltpu.VMEM((n_blocks, 2, 2, 32, 128), f32),
            pltpu.VMEM((n_blocks, 2, 32, 128), f32),
            pltpu.VMEM((n_blocks, 2, 32, 128), f32),
            pltpu.VMEM((N_COL, 32, 128), f32),
            dma((STAGES + 2,)),
            dma((4,)),
            dma((STAGES,)),
            dma((STAGES,)),
            dma((4,)),
            dma((4,)),
            dma((n_blocks,)),
            dma((n_blocks,)),
            dma((n_blocks,)),
            dma,
        ],
        compiler_params=pltpu.CompilerParams(
            collective_id=0, has_side_effects=True, vmem_limit_bytes=60 * 1024 * 1024
        ),
    )(snapshot, basis_two, basis_three)


def solution(mesh):
    in_specs = (P("row", "col", None), P("col", None), P())
    return jax.shard_map(
        on_device, mesh=mesh, in_specs=in_specs, out_specs=P("row", "col"), check_vma=False
    )
```

```python
import jax
import jax.numpy as jnp
from jax import lax
from jax.experimental import pallas as pl
from jax.experimental.pallas import tpu as pltpu
from jax.sharding import PartitionSpec as P

MESH = pl.DeviceIdType.MESH
NT = (((1,), (1,)), ((), ()))

N_COL = 16
PLANES = 8
STAGES = 8
BEHIND = 2
GROUPS = ((0,), (1, 2), (3, 4), (5, 6), (7,))
ROWS = 64 // STAGES
HALF = ROWS // 2
PAIRS = HALF // 2
OFFSETS = (0, -2, -1, 2)
BLOCKS = ((0, 0), (0, 2), (2, 0), (1, 3), (3, 2), (2, 3), (0, 1), (0, 3))


def kernel(
    snap_hbm,
    b2_hbm,
    b3_hbm,
    out_ref,
    snap,
    b3,
    b3t,
    factor,
    weights,
    outgoing,
    incoming,
    pacc,
    half_out,
    rows,
    grams,
    mates,
    sums,
    parts,
    load_sems,
    f_sems,
    a_send,
    a_recv,
    z_send,
    z_recv,
    m_send,
    m_recv,
    g_send,
    g_recv,
):
    row = lax.axis_index("row")
    col = lax.axis_index("col")
    z = row // 2
    xh = lax.rem(row, 2)
    core = lax.rem(col, 2)
    chip = col // 2
    x_lo = lax.rem(chip, 2)
    across = (1 - xh, col ^ 2)

    sign = 1 - 2 * xh

    def plane(offset, away=1):
        return lax.rem(z + away * sign * offset + PLANES, PLANES)

    def remote(src, dst, send_sem, recv_sem, device):
        return pltpu.make_async_remote_copy(
            src_ref=src,
            dst_ref=dst,
            send_sem=send_sem,
            recv_sem=recv_sem,
            device_id=device,
            device_id_type=MESH,
        )

    here = (row, col)
    load_b3 = pltpu.make_async_copy(b3_hbm, b3, load_sems.at[STAGES])
    load_b2 = pltpu.make_async_copy(b2_hbm, factor.at[core, x_lo, chip // 2], load_sems.at[STAGES + 1])
    loads = [
        pltpu.make_async_copy(snap_hbm.at[pl.ds(ROWS * s, ROWS)], snap.at[s], load_sems.at[s])
        for s in range(STAGES)
    ]
    load_b3.start()
    loads[0].start()
    load_b2.start()
    for load in loads[1:]:
        load.start()

    barrier = pltpu.get_barrier_semaphore()

    def greet(device):
        pl.semaphore_signal(barrier, inc=1, device_id=device, device_id_type=MESH)

    def greet_column(i, carry):
        greet((row, col ^ i))
        return carry

    lax.fori_loop(1, N_COL, greet_column, 0)
    for offset in OFFSETS[1:]:
        greet((plane(offset) * 2 + xh, col))
    for offset in OFFSETS:
        greet((plane(offset) * 2 + across[0], across[1]))

    load_b3.wait()
    b3t[...] = b3[...].T

    def first_product(s):
        loads[s].wait()
        left = b3t[...]
        for jp in range(PAIRS):
            j = 2 * jp
            right = jnp.concatenate(
                [snap[s, j], snap[s, HALF + j], snap[s, j + 1], snap[s, HALF + j + 1]], axis=0
            )
            inner = lax.dot_general(left, right, NT, preferred_element_type=jnp.float32)
            pair = jnp.concatenate(
                [inner[:, :128].reshape(N_COL, 8, 128), inner[:, 128:].reshape(N_COL, 8, 128)], axis=1
            ).astype(jnp.bfloat16)
            outgoing[s, :, jp] = pair
        incoming[s, col] = outgoing[s, col ^ (2 * xh)]

    def send_stage(s):
        def body(i, carry):
            peer = col ^ i
            remote(
                outgoing.at[s, peer ^ (2 * xh)], incoming.at[s, col], a_send.at[s], a_recv.at[s], (row, peer)
            ).start()
            return carry

        lax.fori_loop(1, N_COL, body, 0)

    def stage_copy(s):
        most = pl.ds(0, N_COL - 1)
        return remote(outgoing.at[s, most], incoming.at[s, most], a_send.at[s], a_recv.at[s], here)

    first_product(0)
    load_b2.wait()
    pl.semaphore_wait(barrier, N_COL - 1 + 3 + 4)

    own = factor.at[core, x_lo, chip // 2]
    for y in range(1, 4):
        remote(own, own, f_sems.at[0], f_sems.at[1], (row, col ^ (4 * y))).start()
    send_stage(0)
    for s in range(1, STAGES):
        first_product(s)
        send_stage(s)

    most = factor.at[core, x_lo, pl.ds(0, 3)]
    factor_copy = remote(most, most, f_sems.at[0], f_sems.at[1], here)
    factor_copy.wait_recv()
    line = factor.at[core, x_lo]
    other = factor.at[core, 1 - x_lo]
    across_copy = remote(line, line, f_sems.at[4], f_sems.at[5], (z * 2 + across[0], across[1]))
    across_copy.start()
    remote(other, other, f_sems.at[4], f_sems.at[5], here).wait_recv()
    mate = (row, col ^ 1)
    mine = factor.at[core]
    mate_copy = remote(mine, mine, f_sems.at[2], f_sems.at[3], mate)
    mate_copy.start()
    weights[...] = jnp.zeros_like(weights)
    mate_copy.wait_recv()
    for c in range(N_COL):
        block = factor[c % 2, (c // 2) % 2, c // 4]
        weights[pl.ds(c * 128, 64), :128] = block
        weights[pl.ds(c * 128 + 64, 64), 128:] = block

    def send_rows(s):
        for slot, offset in enumerate(OFFSETS):
            if slot:
                to = (plane(offset, -1) * 2 + xh, col)
                remote(rows.at[0, xh, s], rows.at[slot, xh, s], z_send.at[slot], z_recv.at[slot], to).start()
            to = (plane(offset) * 2 + across[0], across[1])
            remote(half_out.at[s], rows.at[slot, xh, s], z_send.at[slot], z_recv.at[slot], to).start()

    def second_product(s):
        stage_copy(s).wait_recv()
        total = jnp.zeros((8 * HALF, 256), jnp.float32)
        for c in range(0, N_COL, 2):
            left = jnp.concatenate(
                [incoming[s, c].reshape(8 * HALF, 128), incoming[s, c + 1].reshape(8 * HALF, 128)], axis=1
            )
            total = total + jnp.dot(left, weights[pl.ds(c * 128, 256), :], preferred_element_type=jnp.float32)
        pacc[0] = total[:, :128]
        pacc[1] = total[:, 128:]
        halves = []
        for h in range(2):
            tiles = []
            for r in range(4 * h, 4 * h + 4):
                every = pl.ds(r, HALF, stride=8)
                tiles.append(jnp.concatenate([pacc[0, every, :], pacc[1, every, :]], axis=0))
            halves.append(
                jnp.concatenate(
                    [jnp.concatenate(tiles[:2], axis=1), jnp.concatenate(tiles[2:], axis=1)], axis=0
                )
            )
        rows[0, xh, s] = jnp.where(xh == 0, halves[0], halves[1]).astype(jnp.bfloat16)
        half_out[s] = jnp.where(xh == 0, halves[1], halves[0]).astype(jnp.bfloat16)

    for s in range(STAGES):
        second_product(s)
        send_rows(s)

    def slot_copy(slot):
        piece = rows.at[slot] if slot else rows.at[0, 0]
        return remote(piece, piece, z_send.at[slot], z_recv.at[slot], here)

    low = lax.broadcasted_iota(jnp.int32, (64, 128), 1) < 64
    sender = xh * 8 + chip

    def mate_gram(b):
        return remote(grams.at[b, 1 - core], mates.at[b], m_send.at[b], m_recv.at[b], mate)

    def gram_copy(b, j):
        slot_u, slot_v = BLOCKS[b]
        to = (plane(OFFSETS[slot_u]) * 2 + core, plane(OFFSETS[slot_v]) * 2 + j)
        own = jnp.logical_and(to[0] == row, to[1] == col)
        return own, remote(sums.at[b, j], parts.at[sender], g_send.at[b], g_recv, to)

    def send_gram(b):
        mate_gram(b).wait_recv()
        sums[b] = grams[b, core] + mates[b]
        for j in range(2):
            own, copy = gram_copy(b, j)

            @pl.when(own)
            def _():
                pltpu.make_async_copy(sums.at[b, j], parts.at[sender], g_recv).start()

            @pl.when(jnp.logical_not(own))
            def _():
                copy.start()

    operands = {}

    def operand(slot):
        if slot not in operands:
            slot_copy(slot).wait_recv()
            whole = rows[slot].reshape(2, STAGES, 2, ROWS, 256)
            flat = jnp.concatenate([whole[:, :, 0].reshape(128, 256), whole[:, :, 1].reshape(128, 256)], axis=1)
            quarters = [flat[32 * i : 32 * i + 32] for i in range(4)]
            operands[slot] = (
                jnp.concatenate([quarters[0], quarters[2]], axis=0),
                jnp.concatenate([quarters[1], quarters[3]], axis=0),
                flat,
                jnp.concatenate([flat[64:], flat[:64]], axis=0),
            )
        return operands[slot]

    def gram_block(b):
        upper, lower, _, _ = operand(BLOCKS[b][0])
        _, _, right, swapped = operand(BLOCKS[b][1])
        m1 = lax.dot_general(upper, right, NT, preferred_element_type=jnp.float32)
        m2 = lax.dot_general(lower, swapped, NT, preferred_element_type=jnp.float32)
        grams[b, :, 0] = jnp.where(low, m1, m2).reshape(2, 32, 128)
        grams[b, :, 1] = jnp.where(low, m2, m1).reshape(2, 32, 128)

    sent = 0
    for group in GROUPS:
        for b in group:
            gram_block(b)
        for b in group:
            mate_gram(b).start()
        while sent < group[0] - BEHIND:
            send_gram(sent)
            sent += 1
    while sent < len(BLOCKS):
        send_gram(sent)
        sent += 1

    pltpu.make_async_copy(parts, parts, g_recv).wait()
    total = jnp.sum(parts[...], axis=0) * (1.0 / 16384.0)
    first, second = total[:, :64], total[:, 64:]
    out_ref[0:32, :] = jnp.where(core == 0, first, second)
    out_ref[32:64, :] = jnp.where(core == 0, second, first)

    factor_copy.wait_send()
    across_copy.wait_send()
    mate_copy.wait_send()
    for s in range(STAGES):
        stage_copy(s).wait_send()
    for slot in range(len(OFFSETS)):
        slot_copy(slot).wait_send()
    for b in range(len(BLOCKS)):
        mate_gram(b).wait_send()
        for j in range(2):
            own, copy = gram_copy(b, j)

            @pl.when(jnp.logical_not(own))
            def _():
                copy.wait_send()


def on_device(snapshot, basis_two, basis_three):
    anywhere = pl.BlockSpec(memory_space=pl.ANY)
    bf16, f32 = jnp.bfloat16, jnp.float32
    dma = pltpu.SemaphoreType.DMA
    n_blocks = len(BLOCKS)
    return pl.pallas_call(
        kernel,
        out_shape=pltpu.VMEM((64, 64), f32),
        in_specs=[anywhere] * 3,
        out_specs=pl.BlockSpec(memory_space=pltpu.VMEM),
        scratch_shapes=[
            pltpu.VMEM((STAGES, ROWS, 64, 512), bf16),
            pltpu.VMEM((512, 128), bf16),
            pltpu.VMEM((128, 512), bf16),
            pltpu.VMEM((2, 2, 4, 64, 128), bf16),
            pltpu.VMEM((N_COL * 128, 256), bf16),
            pltpu.VMEM((STAGES, N_COL, PAIRS, 16, 128), bf16),
            pltpu.VMEM((STAGES, N_COL, PAIRS, 16, 128), bf16),
            pltpu.VMEM((2, 8 * HALF, 128), f32),
            pltpu.VMEM((STAGES, 2 * ROWS, 256), bf16),
            pltpu.VMEM((4, 2, STAGES, 2 * ROWS, 256), bf16),
            pltpu.VMEM((n_blocks, 2, 2, 32, 128), f32),
            pltpu.VMEM((n_blocks, 2, 32, 128), f32),
            pltpu.VMEM((n_blocks, 2, 32, 128), f32),
            pltpu.VMEM((N_COL, 32, 128), f32),
            dma((STAGES + 2,)),
            dma((6,)),
            dma((STAGES,)),
            dma((STAGES,)),
            dma((4,)),
            dma((4,)),
            dma((n_blocks,)),
            dma((n_blocks,)),
            dma((n_blocks,)),
            dma,
        ],
        compiler_params=pltpu.CompilerParams(
            collective_id=0, has_side_effects=True, vmem_limit_bytes=60 * 1024 * 1024
        ),
    )(snapshot, basis_two, basis_three)


def solution(mesh):
    in_specs = (P("row", "col", None), P("col", None), P())
    return jax.shard_map(
        on_device, mesh=mesh, in_specs=in_specs, out_specs=P("row", "col"), check_vma=False
    )
```

```python
import jax
import jax.numpy as jnp
from jax import lax
from jax.experimental import pallas as pl
from jax.experimental.pallas import tpu as pltpu
from jax.sharding import PartitionSpec as P

MESH = pl.DeviceIdType.MESH
NT = (((1,), (1,)), ((), ()))

N_COL = 16
PLANES = 8
STAGES = 8
BEHIND = 2
EAGER = 2
GROUPS = ((0,), (1, 2), (3, 4), (5, 6), (7,))
ROWS = 64 // STAGES
HALF = ROWS // 2
PAIRS = HALF // 2
OFFSETS = (0, -2, -1, 2)
BLOCKS = ((0, 0), (0, 2), (2, 0), (0, 1), (0, 3), (1, 3), (3, 2), (2, 3))


def kernel(
    snap_hbm,
    b2_hbm,
    b3_hbm,
    out_ref,
    snap,
    b3,
    b3t,
    factor,
    weights,
    outgoing,
    incoming,
    pacc,
    half_out,
    rows,
    grams,
    mates,
    sums,
    parts,
    load_sems,
    f_sems,
    a_send,
    a_recv,
    z_send,
    z_recv,
    m_send,
    m_recv,
    g_send,
    g_recv,
    ready,
):
    row = lax.axis_index("row")
    col = lax.axis_index("col")
    z = row // 2
    xh = lax.rem(row, 2)
    core = lax.rem(col, 2)
    chip = col // 2
    x_lo = lax.rem(chip, 2)
    across = (1 - xh, col ^ 2)

    sign = 1 - 2 * xh

    def plane(offset, away=1):
        return lax.rem(z + away * sign * offset + PLANES, PLANES)

    def remote(src, dst, send_sem, recv_sem, device):
        return pltpu.make_async_remote_copy(
            src_ref=src,
            dst_ref=dst,
            send_sem=send_sem,
            recv_sem=recv_sem,
            device_id=device,
            device_id_type=MESH,
        )

    here = (row, col)
    load_b3 = pltpu.make_async_copy(b3_hbm, b3, load_sems.at[STAGES])
    load_b2 = pltpu.make_async_copy(b2_hbm, factor.at[core, x_lo, chip // 2], load_sems.at[STAGES + 1])
    loads = [
        pltpu.make_async_copy(snap_hbm.at[pl.ds(ROWS * s, ROWS)], snap.at[s], load_sems.at[s])
        for s in range(STAGES)
    ]
    load_b3.start()
    loads[0].start()
    load_b2.start()
    for load in loads[1:]:
        load.start()

    barrier = pltpu.get_barrier_semaphore()

    def greet(device):
        pl.semaphore_signal(barrier, inc=1, device_id=device, device_id_type=MESH)

    def greet_column(i, carry):
        greet((row, col ^ i))
        return carry

    lax.fori_loop(1, N_COL, greet_column, 0)
    greet((z * 2 + across[0], across[1]))

    edges = []
    for slot, offset in enumerate(OFFSETS):
        if slot:
            edges.append((plane(offset, -1), plane(offset), (xh, col)))
            edges.append((plane(offset), plane(offset), across))

    def where(test):
        return jnp.where(test, 1, 0)

    greetings, answers = N_COL, 0
    for target, source, (there, at) in edges:

        @pl.when(target > z)
        def _():
            greet((target * 2 + there, at))

        @pl.when(source > z)
        def _():
            greet((source * 2 + there, at))

        greetings = greetings + where(target < z) + where(source < z)
        answers = answers + where(target > z)

    load_b3.wait()
    b3t[...] = b3[...].T

    def first_product(s):
        loads[s].wait()
        left = b3t[...]
        for jp in range(PAIRS):
            j = 2 * jp
            right = jnp.concatenate(
                [snap[s, j], snap[s, HALF + j], snap[s, j + 1], snap[s, HALF + j + 1]], axis=0
            )
            inner = lax.dot_general(left, right, NT, preferred_element_type=jnp.float32)
            pair = jnp.concatenate(
                [inner[:, :128].reshape(N_COL, 8, 128), inner[:, 128:].reshape(N_COL, 8, 128)], axis=1
            ).astype(jnp.bfloat16)
            outgoing[s, :, jp] = pair
        incoming[s, col] = outgoing[s, col ^ (2 * xh)]

    def send_stage(s):
        def body(i, carry):
            peer = col ^ i
            remote(
                outgoing.at[s, peer ^ (2 * xh)], incoming.at[s, col], a_send.at[s], a_recv.at[s], (row, peer)
            ).start()
            return carry

        lax.fori_loop(1, N_COL, body, 0)

    def stage_copy(s):
        most = pl.ds(0, N_COL - 1)
        return remote(outgoing.at[s, most], incoming.at[s, most], a_send.at[s], a_recv.at[s], here)

    first_product(0)
    load_b2.wait()
    pl.semaphore_wait(barrier, greetings)
    for _, source, (there, at) in edges:

        @pl.when(source < z)
        def _():
            pl.semaphore_signal(ready, inc=1, device_id=(source * 2 + there, at), device_id_type=MESH)


    own = factor.at[core, x_lo, chip // 2]
    for y in range(1, 4):
        remote(own, own, f_sems.at[0], f_sems.at[1], (row, col ^ (4 * y))).start()
    send_stage(0)
    for s in range(1, STAGES):
        first_product(s)
        send_stage(s)

    most = factor.at[core, x_lo, pl.ds(0, 3)]
    factor_copy = remote(most, most, f_sems.at[0], f_sems.at[1], here)
    factor_copy.wait_recv()
    line = factor.at[core, x_lo]
    other = factor.at[core, 1 - x_lo]
    across_copy = remote(line, line, f_sems.at[4], f_sems.at[5], (z * 2 + across[0], across[1]))
    across_copy.start()
    remote(other, other, f_sems.at[4], f_sems.at[5], here).wait_recv()
    mate = (row, col ^ 1)
    mine = factor.at[core]
    mate_copy = remote(mine, mine, f_sems.at[2], f_sems.at[3], mate)
    mate_copy.start()
    weights[...] = jnp.zeros_like(weights)
    mate_copy.wait_recv()
    for c in range(N_COL):
        block = factor[c % 2, (c // 2) % 2, c // 4]
        weights[pl.ds(c * 128, 64), :128] = block
        weights[pl.ds(c * 128 + 64, 64), 128:] = block

    def send_rows(s):
        for slot, offset in enumerate(OFFSETS):
            if slot:
                to = (plane(offset, -1) * 2 + xh, col)
                remote(rows.at[0, xh, s], rows.at[slot, xh, s], z_send.at[slot], z_recv.at[slot], to).start()
            to = (plane(offset) * 2 + across[0], across[1])
            remote(half_out.at[s], rows.at[slot, xh, s], z_send.at[slot], z_recv.at[slot], to).start()

    def second_product(s):
        stage_copy(s).wait_recv()
        total = jnp.zeros((8 * HALF, 256), jnp.float32)
        for c in range(0, N_COL, 2):
            left = jnp.concatenate(
                [incoming[s, c].reshape(8 * HALF, 128), incoming[s, c + 1].reshape(8 * HALF, 128)], axis=1
            )
            total = total + jnp.dot(left, weights[pl.ds(c * 128, 256), :], preferred_element_type=jnp.float32)
        pacc[0] = total[:, :128]
        pacc[1] = total[:, 128:]
        halves = []
        for h in range(2):
            tiles = []
            for r in range(4 * h, 4 * h + 4):
                every = pl.ds(r, HALF, stride=8)
                tiles.append(jnp.concatenate([pacc[0, every, :], pacc[1, every, :]], axis=0))
            halves.append(
                jnp.concatenate(
                    [jnp.concatenate(tiles[:2], axis=1), jnp.concatenate(tiles[2:], axis=1)], axis=0
                )
            )
        rows[0, xh, s] = jnp.where(xh == 0, halves[0], halves[1]).astype(jnp.bfloat16)
        half_out[s] = jnp.where(xh == 0, halves[1], halves[0]).astype(jnp.bfloat16)

    @pl.when(answers > 0)
    def _():
        pl.semaphore_wait(ready, answers)

    for s in range(STAGES):
        second_product(s)
        send_rows(s)

    def slot_copy(slot):
        piece = rows.at[slot] if slot else rows.at[0, 0]
        return remote(piece, piece, z_send.at[slot], z_recv.at[slot], here)

    low = lax.broadcasted_iota(jnp.int32, (64, 128), 1) < 64
    sender = xh * 8 + chip

    def mate_gram(b):
        return remote(grams.at[b, 1 - core], mates.at[b], m_send.at[b], m_recv.at[b], mate)

    def gram_copy(b, j):
        slot_u, slot_v = BLOCKS[b]
        to = (plane(OFFSETS[slot_u]) * 2 + core, plane(OFFSETS[slot_v]) * 2 + j)
        own = jnp.logical_and(to[0] == row, to[1] == col)
        return own, remote(sums.at[b, j], parts.at[sender], g_send.at[b], g_recv, to)

    def send_gram(b):
        mate_gram(b).wait_recv()
        sums[b] = grams[b, core] + mates[b]
        for j in range(2):
            own, copy = gram_copy(b, j)

            @pl.when(own)
            def _():
                pltpu.make_async_copy(sums.at[b, j], parts.at[sender], g_recv).start()

            @pl.when(jnp.logical_not(own))
            def _():
                copy.start()

    operands = {}

    def operand(slot):
        if slot not in operands:
            slot_copy(slot).wait_recv()
            whole = rows[slot].reshape(2, STAGES, 2, ROWS, 256)
            flat = jnp.concatenate([whole[:, :, 0].reshape(128, 256), whole[:, :, 1].reshape(128, 256)], axis=1)
            quarters = [flat[32 * i : 32 * i + 32] for i in range(4)]
            operands[slot] = (
                jnp.concatenate([quarters[0], quarters[2]], axis=0),
                jnp.concatenate([quarters[1], quarters[3]], axis=0),
                flat,
                jnp.concatenate([flat[64:], flat[:64]], axis=0),
            )
        return operands[slot]

    def gram_block(b):
        upper, lower, _, _ = operand(BLOCKS[b][0])
        _, _, right, swapped = operand(BLOCKS[b][1])
        m1 = lax.dot_general(upper, right, NT, preferred_element_type=jnp.float32)
        m2 = lax.dot_general(lower, swapped, NT, preferred_element_type=jnp.float32)
        grams[b, :, 0] = jnp.where(low, m1, m2).reshape(2, 32, 128)
        grams[b, :, 1] = jnp.where(low, m2, m1).reshape(2, 32, 128)

    sent = 0
    for turn, group in enumerate(GROUPS):
        for b in group:
            gram_block(b)
        for b in group:
            mate_gram(b).start()
        while sent < (group[-1] + 1 if turn < EAGER else group[0] - BEHIND):
            send_gram(sent)
            sent += 1
    while sent < len(BLOCKS):
        send_gram(sent)
        sent += 1

    pltpu.make_async_copy(parts, parts, g_recv).wait()
    total = jnp.sum(parts[...], axis=0) * (1.0 / 16384.0)
    first, second = total[:, :64], total[:, 64:]
    out_ref[0:32, :] = jnp.where(core == 0, first, second)
    out_ref[32:64, :] = jnp.where(core == 0, second, first)

    factor_copy.wait_send()
    across_copy.wait_send()
    mate_copy.wait_send()
    for s in range(STAGES):
        stage_copy(s).wait_send()
    for slot in range(len(OFFSETS)):
        slot_copy(slot).wait_send()
    for b in range(len(BLOCKS)):
        mate_gram(b).wait_send()
        for j in range(2):
            own, copy = gram_copy(b, j)

            @pl.when(jnp.logical_not(own))
            def _():
                copy.wait_send()


def on_device(snapshot, basis_two, basis_three):
    anywhere = pl.BlockSpec(memory_space=pl.ANY)
    bf16, f32 = jnp.bfloat16, jnp.float32
    dma = pltpu.SemaphoreType.DMA
    n_blocks = len(BLOCKS)
    return pl.pallas_call(
        kernel,
        out_shape=pltpu.VMEM((64, 64), f32),
        in_specs=[anywhere] * 3,
        out_specs=pl.BlockSpec(memory_space=pltpu.VMEM),
        scratch_shapes=[
            pltpu.VMEM((STAGES, ROWS, 64, 512), bf16),
            pltpu.VMEM((512, 128), bf16),
            pltpu.VMEM((128, 512), bf16),
            pltpu.VMEM((2, 2, 4, 64, 128), bf16),
            pltpu.VMEM((N_COL * 128, 256), bf16),
            pltpu.VMEM((STAGES, N_COL, PAIRS, 16, 128), bf16),
            pltpu.VMEM((STAGES, N_COL, PAIRS, 16, 128), bf16),
            pltpu.VMEM((2, 8 * HALF, 128), f32),
            pltpu.VMEM((STAGES, 2 * ROWS, 256), bf16),
            pltpu.VMEM((4, 2, STAGES, 2 * ROWS, 256), bf16),
            pltpu.VMEM((n_blocks, 2, 2, 32, 128), f32),
            pltpu.VMEM((n_blocks, 2, 32, 128), f32),
            pltpu.VMEM((n_blocks, 2, 32, 128), f32),
            pltpu.VMEM((N_COL, 32, 128), f32),
            dma((STAGES + 2,)),
            dma((6,)),
            dma((STAGES,)),
            dma((STAGES,)),
            dma((4,)),
            dma((4,)),
            dma((n_blocks,)),
            dma((n_blocks,)),
            dma((n_blocks,)),
            dma,
            pltpu.SemaphoreType.REGULAR,
        ],
        compiler_params=pltpu.CompilerParams(
            collective_id=0, has_side_effects=True, vmem_limit_bytes=60 * 1024 * 1024
        ),
    )(snapshot, basis_two, basis_three)


def solution(mesh):
    in_specs = (P("row", "col", None), P("col", None), P())
    return jax.shard_map(
        on_device, mesh=mesh, in_specs=in_specs, out_specs=P("row", "col"), check_vma=False
    )
```

```python
import jax
import jax.numpy as jnp
from jax import lax
from jax.experimental import pallas as pl
from jax.experimental.pallas import tpu as pltpu
from jax.sharding import PartitionSpec as P

MESH = pl.DeviceIdType.MESH
NT = (((1,), (1,)), ((), ()))

N_COL = 16
PLANES = 8
STAGES = 8
BEHIND = 2
GROUPS = ((0,), (1, 2), (3, 4), (5, 6), (7,))
GROUPS_UP = ((0,), (4,), (1, 2), (3, 5), (6, 7))
GROUPS_DOWN = ((0,), (1, 2), (3,), (4, 5), (6, 7))
ROWS = 64 // STAGES
HALF = ROWS // 2
PAIRS = HALF // 2
OFFSETS = (0, -2, -1, 2)
BLOCKS = ((0, 0), (0, 2), (2, 0), (0, 1), (0, 3), (1, 3), (3, 2), (2, 3))


def kernel(
    snap_hbm,
    b2_hbm,
    b3_hbm,
    out_ref,
    snap,
    b3,
    b3t,
    factor,
    weights,
    outgoing,
    incoming,
    pacc,
    half_out,
    rows,
    grams,
    mates,
    sums,
    parts,
    load_sems,
    f_sems,
    a_send,
    a_recv,
    z_send,
    z_recv,
    m_send,
    m_recv,
    g_send,
    g_recv,
    ready,
):
    row = lax.axis_index("row")
    col = lax.axis_index("col")
    z = row // 2
    xh = lax.rem(row, 2)
    core = lax.rem(col, 2)
    chip = col // 2
    x_lo = lax.rem(chip, 2)
    across = (1 - xh, col ^ 2)

    sign = 1 - 2 * xh

    def plane(offset, away=1):
        return lax.rem(z + away * sign * offset + PLANES, PLANES)

    def remote(src, dst, send_sem, recv_sem, device):
        return pltpu.make_async_remote_copy(
            src_ref=src,
            dst_ref=dst,
            send_sem=send_sem,
            recv_sem=recv_sem,
            device_id=device,
            device_id_type=MESH,
        )

    here = (row, col)
    load_b3 = pltpu.make_async_copy(b3_hbm, b3, load_sems.at[STAGES])
    load_b2 = pltpu.make_async_copy(b2_hbm, factor.at[core, x_lo, chip // 2], load_sems.at[STAGES + 1])
    loads = [
        pltpu.make_async_copy(snap_hbm.at[pl.ds(ROWS * s, ROWS)], snap.at[s], load_sems.at[s])
        for s in range(STAGES)
    ]
    load_b3.start()
    loads[0].start()
    load_b2.start()
    for load in loads[1:]:
        load.start()

    barrier = pltpu.get_barrier_semaphore()

    def greet(device):
        pl.semaphore_signal(barrier, inc=1, device_id=device, device_id_type=MESH)

    def greet_column(i, carry):
        greet((row, col ^ i))
        return carry

    lax.fori_loop(1, N_COL, greet_column, 0)
    greet((z * 2 + across[0], across[1]))

    edges = []
    for slot, offset in enumerate(OFFSETS):
        if slot:
            edges.append((plane(offset, -1), plane(offset), (xh, col)))
            edges.append((plane(offset), plane(offset), across))

    def where(test):
        return jnp.where(test, 1, 0)

    greetings, answers = N_COL, 0
    for target, source, (there, at) in edges:

        @pl.when(target > z)
        def _():
            greet((target * 2 + there, at))

        @pl.when(source > z)
        def _():
            greet((source * 2 + there, at))

        greetings = greetings + where(target < z) + where(source < z)
        answers = answers + where(target > z)

    load_b3.wait()
    b3t[...] = b3[...].T

    def first_product(s):
        loads[s].wait()
        left = b3t[...]
        for jp in range(PAIRS):
            j = 2 * jp
            right = jnp.concatenate(
                [snap[s, j], snap[s, HALF + j], snap[s, j + 1], snap[s, HALF + j + 1]], axis=0
            )
            inner = lax.dot_general(left, right, NT, preferred_element_type=jnp.float32)
            pair = jnp.concatenate(
                [inner[:, :128].reshape(N_COL, 8, 128), inner[:, 128:].reshape(N_COL, 8, 128)], axis=1
            ).astype(jnp.bfloat16)
            outgoing[s, :, jp] = pair
        incoming[s, col] = outgoing[s, col ^ (2 * xh)]

    def send_stage(s):
        def body(i, carry):
            peer = col ^ i
            remote(
                outgoing.at[s, peer ^ (2 * xh)], incoming.at[s, col], a_send.at[s], a_recv.at[s], (row, peer)
            ).start()
            return carry

        lax.fori_loop(1, N_COL, body, 0)

    def stage_copy(s):
        most = pl.ds(0, N_COL - 1)
        return remote(outgoing.at[s, most], incoming.at[s, most], a_send.at[s], a_recv.at[s], here)

    first_product(0)
    load_b2.wait()
    pl.semaphore_wait(barrier, greetings)
    for _, source, (there, at) in edges:

        @pl.when(source < z)
        def _():
            pl.semaphore_signal(ready, inc=1, device_id=(source * 2 + there, at), device_id_type=MESH)


    own = factor.at[core, x_lo, chip // 2]
    for y in range(1, 4):
        remote(own, own, f_sems.at[0], f_sems.at[1], (row, col ^ (4 * y))).start()
    send_stage(0)
    for s in range(1, STAGES):
        first_product(s)
        send_stage(s)

    most = factor.at[core, x_lo, pl.ds(0, 3)]
    factor_copy = remote(most, most, f_sems.at[0], f_sems.at[1], here)
    factor_copy.wait_recv()
    line = factor.at[core, x_lo]
    other = factor.at[core, 1 - x_lo]
    across_copy = remote(line, line, f_sems.at[4], f_sems.at[5], (z * 2 + across[0], across[1]))
    across_copy.start()
    remote(other, other, f_sems.at[4], f_sems.at[5], here).wait_recv()
    mate = (row, col ^ 1)
    mine = factor.at[core]
    mate_copy = remote(mine, mine, f_sems.at[2], f_sems.at[3], mate)
    mate_copy.start()
    weights[...] = jnp.zeros_like(weights)
    mate_copy.wait_recv()
    for c in range(N_COL):
        block = factor[c % 2, (c // 2) % 2, c // 4]
        weights[pl.ds(c * 128, 64), :128] = block
        weights[pl.ds(c * 128 + 64, 64), 128:] = block

    def send_rows(s):
        for slot, offset in enumerate(OFFSETS):
            if slot:
                to = (plane(offset, -1) * 2 + xh, col)
                remote(rows.at[0, xh, s], rows.at[slot, xh, s], z_send.at[slot], z_recv.at[slot], to).start()
            to = (plane(offset) * 2 + across[0], across[1])
            remote(half_out.at[s], rows.at[slot, xh, s], z_send.at[slot], z_recv.at[slot], to).start()

    def second_product(s):
        stage_copy(s).wait_recv()
        total = jnp.zeros((8 * HALF, 256), jnp.float32)
        for c in range(0, N_COL, 2):
            left = jnp.concatenate(
                [incoming[s, c].reshape(8 * HALF, 128), incoming[s, c + 1].reshape(8 * HALF, 128)], axis=1
            )
            total = total + jnp.dot(left, weights[pl.ds(c * 128, 256), :], preferred_element_type=jnp.float32)
        pacc[0] = total[:, :128]
        pacc[1] = total[:, 128:]
        halves = []
        for h in range(2):
            tiles = []
            for r in range(4 * h, 4 * h + 4):
                every = pl.ds(r, HALF, stride=8)
                tiles.append(jnp.concatenate([pacc[0, every, :], pacc[1, every, :]], axis=0))
            halves.append(
                jnp.concatenate(
                    [jnp.concatenate(tiles[:2], axis=1), jnp.concatenate(tiles[2:], axis=1)], axis=0
                )
            )
        rows[0, xh, s] = jnp.where(xh == 0, halves[0], halves[1]).astype(jnp.bfloat16)
        half_out[s] = jnp.where(xh == 0, halves[1], halves[0]).astype(jnp.bfloat16)

    @pl.when(answers > 0)
    def _():
        pl.semaphore_wait(ready, answers)

    for s in range(STAGES):
        second_product(s)
        send_rows(s)

    def slot_copy(slot):
        piece = rows.at[slot] if slot else rows.at[0, 0]
        return remote(piece, piece, z_send.at[slot], z_recv.at[slot], here)

    low = lax.broadcasted_iota(jnp.int32, (64, 128), 1) < 64
    sender = xh * 8 + chip

    def mate_gram(b):
        return remote(grams.at[b, 1 - core], mates.at[b], m_send.at[b], m_recv.at[b], mate)

    def gram_copy(b, j):
        slot_u, slot_v = BLOCKS[b]
        to = (plane(OFFSETS[slot_u]) * 2 + core, plane(OFFSETS[slot_v]) * 2 + j)
        own = jnp.logical_and(to[0] == row, to[1] == col)
        return own, remote(sums.at[b, j], parts.at[sender], g_send.at[b], g_recv, to)

    def send_gram(b):
        mate_gram(b).wait_recv()
        sums[b] = grams[b, core] + mates[b]
        for j in range(2):
            own, copy = gram_copy(b, j)

            @pl.when(own)
            def _():
                pltpu.make_async_copy(sums.at[b, j], parts.at[sender], g_recv).start()

            @pl.when(jnp.logical_not(own))
            def _():
                copy.start()

    operands = {}

    def operand(slot):
        if slot not in operands:
            slot_copy(slot).wait_recv()
            whole = rows[slot].reshape(2, STAGES, 2, ROWS, 256)
            flat = jnp.concatenate([whole[:, :, 0].reshape(128, 256), whole[:, :, 1].reshape(128, 256)], axis=1)
            quarters = [flat[32 * i : 32 * i + 32] for i in range(4)]
            operands[slot] = (
                jnp.concatenate([quarters[0], quarters[2]], axis=0),
                jnp.concatenate([quarters[1], quarters[3]], axis=0),
                flat,
                jnp.concatenate([flat[64:], flat[:64]], axis=0),
            )
        return operands[slot]

    def gram_block(b):
        upper, lower, _, _ = operand(BLOCKS[b][0])
        _, _, right, swapped = operand(BLOCKS[b][1])
        m1 = lax.dot_general(upper, right, NT, preferred_element_type=jnp.float32)
        m2 = lax.dot_general(lower, swapped, NT, preferred_element_type=jnp.float32)
        grams[b, :, 0] = jnp.where(low, m1, m2).reshape(2, 32, 128)
        grams[b, :, 1] = jnp.where(low, m2, m1).reshape(2, 32, 128)

    def work_through(groups, eager):
        operands.clear()
        order = [b for group in groups for b in group]
        sent = begun = 0
        for turn, group in enumerate(groups):
            for b in group:
                gram_block(b)
            for b in group:
                mate_gram(b).start()
            ready_to_send = begun + len(group) if turn < eager else begun - BEHIND
            begun += len(group)
            while sent < ready_to_send:
                send_gram(order[sent])
                sent += 1
        for b in order[sent:]:
            send_gram(b)

    first_up = jnp.logical_and(z == 0, xh == 0)
    first_down = jnp.logical_and(z == 0, xh == 1)

    @pl.when(first_up)
    def _():
        work_through(GROUPS_UP, 2)

    @pl.when(first_down)
    def _():
        work_through(GROUPS_DOWN, 3)

    @pl.when(z > 0)
    def _():
        work_through(GROUPS, 2)

    pltpu.make_async_copy(parts, parts, g_recv).wait()
    total = jnp.sum(parts[...], axis=0) * (1.0 / 16384.0)
    first, second = total[:, :64], total[:, 64:]
    out_ref[0:32, :] = jnp.where(core == 0, first, second)
    out_ref[32:64, :] = jnp.where(core == 0, second, first)

    factor_copy.wait_send()
    across_copy.wait_send()
    mate_copy.wait_send()
    for s in range(STAGES):
        stage_copy(s).wait_send()
    for slot in range(len(OFFSETS)):
        slot_copy(slot).wait_send()
    for b in range(len(BLOCKS)):
        mate_gram(b).wait_send()
        for j in range(2):
            own, copy = gram_copy(b, j)

            @pl.when(jnp.logical_not(own))
            def _():
                copy.wait_send()


def on_device(snapshot, basis_two, basis_three):
    anywhere = pl.BlockSpec(memory_space=pl.ANY)
    bf16, f32 = jnp.bfloat16, jnp.float32
    dma = pltpu.SemaphoreType.DMA
    n_blocks = len(BLOCKS)
    return pl.pallas_call(
        kernel,
        out_shape=pltpu.VMEM((64, 64), f32),
        in_specs=[anywhere] * 3,
        out_specs=pl.BlockSpec(memory_space=pltpu.VMEM),
        scratch_shapes=[
            pltpu.VMEM((STAGES, ROWS, 64, 512), bf16),
            pltpu.VMEM((512, 128), bf16),
            pltpu.VMEM((128, 512), bf16),
            pltpu.VMEM((2, 2, 4, 64, 128), bf16),
            pltpu.VMEM((N_COL * 128, 256), bf16),
            pltpu.VMEM((STAGES, N_COL, PAIRS, 16, 128), bf16),
            pltpu.VMEM((STAGES, N_COL, PAIRS, 16, 128), bf16),
            pltpu.VMEM((2, 8 * HALF, 128), f32),
            pltpu.VMEM((STAGES, 2 * ROWS, 256), bf16),
            pltpu.VMEM((4, 2, STAGES, 2 * ROWS, 256), bf16),
            pltpu.VMEM((n_blocks, 2, 2, 32, 128), f32),
            pltpu.VMEM((n_blocks, 2, 32, 128), f32),
            pltpu.VMEM((n_blocks, 2, 32, 128), f32),
            pltpu.VMEM((N_COL, 32, 128), f32),
            dma((STAGES + 2,)),
            dma((6,)),
            dma((STAGES,)),
            dma((STAGES,)),
            dma((4,)),
            dma((4,)),
            dma((n_blocks,)),
            dma((n_blocks,)),
            dma((n_blocks,)),
            dma,
            pltpu.SemaphoreType.REGULAR,
        ],
        compiler_params=pltpu.CompilerParams(
            collective_id=0, has_side_effects=True, vmem_limit_bytes=60 * 1024 * 1024
        ),
    )(snapshot, basis_two, basis_three)


def solution(mesh):
    in_specs = (P("row", "col", None), P("col", None), P())
    return jax.shard_map(
        on_device, mesh=mesh, in_specs=in_specs, out_specs=P("row", "col"), check_vma=False
    )
```

```python
import jax
import jax.numpy as jnp
from jax import lax
from jax.experimental import pallas as pl
from jax.experimental.pallas import tpu as pltpu
from jax.sharding import PartitionSpec as P

MESH = pl.DeviceIdType.MESH
NT = (((1,), (1,)), ((), ()))

N_COL = 16
PLANES = 8
STAGES = 8
BEHIND = 2
GROUPS = ((0,), (1, 2), (3, 4), (5, 6), (7,))
GROUPS_NEXT = ((0,), (1, 2), (4,), (6, 7), (3, 5))
GROUPS_UP = ((0,), (4,), (1, 2), (3, 5), (6, 7))
GROUPS_DOWN = ((0,), (1, 2), (3,), (4, 5), (6, 7))
ROWS = 64 // STAGES
HALF = ROWS // 2
PAIRS = HALF // 2
OFFSETS = (0, -2, -1, 2)
BLOCKS = ((0, 0), (0, 2), (2, 0), (0, 1), (0, 3), (1, 3), (3, 2), (2, 3))


def kernel(
    snap_hbm,
    b2_hbm,
    b3_hbm,
    out_ref,
    snap,
    b3,
    b3t,
    factor,
    weights,
    outgoing,
    incoming,
    pacc,
    half_out,
    rows,
    grams,
    mates,
    sums,
    parts,
    load_sems,
    f_sems,
    a_send,
    a_recv,
    z_send,
    z_recv,
    m_send,
    m_recv,
    g_send,
    g_recv,
    ready,
):
    row = lax.axis_index("row")
    col = lax.axis_index("col")
    z = row // 2
    xh = lax.rem(row, 2)
    core = lax.rem(col, 2)
    chip = col // 2
    x_lo = lax.rem(chip, 2)
    across = (1 - xh, col ^ 2)

    sign = 1 - 2 * xh

    def plane(offset, away=1):
        return lax.rem(z + away * sign * offset + PLANES, PLANES)

    def remote(src, dst, send_sem, recv_sem, device):
        return pltpu.make_async_remote_copy(
            src_ref=src,
            dst_ref=dst,
            send_sem=send_sem,
            recv_sem=recv_sem,
            device_id=device,
            device_id_type=MESH,
        )

    here = (row, col)
    load_b3 = pltpu.make_async_copy(b3_hbm, b3, load_sems.at[STAGES])
    load_b2 = pltpu.make_async_copy(b2_hbm, factor.at[core, x_lo, chip // 2], load_sems.at[STAGES + 1])
    loads = [
        pltpu.make_async_copy(snap_hbm.at[pl.ds(ROWS * s, ROWS)], snap.at[s], load_sems.at[s])
        for s in range(STAGES)
    ]
    load_b3.start()
    loads[0].start()
    load_b2.start()
    for load in loads[1:]:
        load.start()

    barrier = pltpu.get_barrier_semaphore()

    def greet(device):
        pl.semaphore_signal(barrier, inc=1, device_id=device, device_id_type=MESH)

    def greet_column(i, carry):
        greet((row, col ^ i))
        return carry

    lax.fori_loop(1, N_COL, greet_column, 0)
    greet((z * 2 + across[0], across[1]))

    edges = []
    for slot, offset in enumerate(OFFSETS):
        if slot:
            edges.append((plane(offset, -1), plane(offset), (xh, col)))
            edges.append((plane(offset), plane(offset), across))

    def where(test):
        return jnp.where(test, 1, 0)

    greetings, answers = N_COL, 0
    for target, source, (there, at) in edges:

        @pl.when(target > z)
        def _():
            greet((target * 2 + there, at))

        @pl.when(source > z)
        def _():
            greet((source * 2 + there, at))

        greetings = greetings + where(target < z) + where(source < z)
        answers = answers + where(target > z)

    load_b3.wait()
    b3t[...] = b3[...].T

    def first_product(s):
        loads[s].wait()
        left = b3t[...]
        for jp in range(PAIRS):
            j = 2 * jp
            right = jnp.concatenate(
                [snap[s, j], snap[s, HALF + j], snap[s, j + 1], snap[s, HALF + j + 1]], axis=0
            )
            inner = lax.dot_general(left, right, NT, preferred_element_type=jnp.float32)
            pair = jnp.concatenate(
                [inner[:, :128].reshape(N_COL, 8, 128), inner[:, 128:].reshape(N_COL, 8, 128)], axis=1
            ).astype(jnp.bfloat16)
            outgoing[s, :, jp] = pair
        incoming[s, col] = outgoing[s, col ^ (2 * xh)]

    def send_stage(s):
        def body(i, carry):
            peer = col ^ i
            remote(
                outgoing.at[s, peer ^ (2 * xh)], incoming.at[s, col], a_send.at[s], a_recv.at[s], (row, peer)
            ).start()
            return carry

        lax.fori_loop(1, N_COL, body, 0)

    def stage_copy(s):
        most = pl.ds(0, N_COL - 1)
        return remote(outgoing.at[s, most], incoming.at[s, most], a_send.at[s], a_recv.at[s], here)

    first_product(0)
    load_b2.wait()
    pl.semaphore_wait(barrier, greetings)
    for _, source, (there, at) in edges:

        @pl.when(source < z)
        def _():
            pl.semaphore_signal(ready, inc=1, device_id=(source * 2 + there, at), device_id_type=MESH)


    own = factor.at[core, x_lo, chip // 2]
    for y in range(1, 4):
        remote(own, own, f_sems.at[0], f_sems.at[1], (row, col ^ (4 * y))).start()
    send_stage(0)
    for s in range(1, STAGES):
        first_product(s)
        send_stage(s)

    most = factor.at[core, x_lo, pl.ds(0, 3)]
    factor_copy = remote(most, most, f_sems.at[0], f_sems.at[1], here)
    factor_copy.wait_recv()
    line = factor.at[core, x_lo]
    other = factor.at[core, 1 - x_lo]
    across_copy = remote(line, line, f_sems.at[4], f_sems.at[5], (z * 2 + across[0], across[1]))
    across_copy.start()
    remote(other, other, f_sems.at[4], f_sems.at[5], here).wait_recv()
    mate = (row, col ^ 1)
    mine = factor.at[core]
    mate_copy = remote(mine, mine, f_sems.at[2], f_sems.at[3], mate)
    mate_copy.start()
    weights[...] = jnp.zeros_like(weights)
    mate_copy.wait_recv()
    for c in range(N_COL):
        block = factor[c % 2, (c // 2) % 2, c // 4]
        weights[pl.ds(c * 128, 64), :128] = block
        weights[pl.ds(c * 128 + 64, 64), 128:] = block

    def send_rows(s):
        for slot, offset in enumerate(OFFSETS):
            if slot:
                to = (plane(offset, -1) * 2 + xh, col)
                remote(rows.at[0, xh, s], rows.at[slot, xh, s], z_send.at[slot], z_recv.at[slot], to).start()
            to = (plane(offset) * 2 + across[0], across[1])
            remote(half_out.at[s], rows.at[slot, xh, s], z_send.at[slot], z_recv.at[slot], to).start()

    def second_product(s):
        stage_copy(s).wait_recv()
        total = jnp.zeros((8 * HALF, 256), jnp.float32)
        for c in range(0, N_COL, 2):
            left = jnp.concatenate(
                [incoming[s, c].reshape(8 * HALF, 128), incoming[s, c + 1].reshape(8 * HALF, 128)], axis=1
            )
            total = total + jnp.dot(left, weights[pl.ds(c * 128, 256), :], preferred_element_type=jnp.float32)
        pacc[0] = total[:, :128]
        pacc[1] = total[:, 128:]
        halves = []
        for h in range(2):
            tiles = []
            for r in range(4 * h, 4 * h + 4):
                every = pl.ds(r, HALF, stride=8)
                tiles.append(jnp.concatenate([pacc[0, every, :], pacc[1, every, :]], axis=0))
            halves.append(
                jnp.concatenate(
                    [jnp.concatenate(tiles[:2], axis=1), jnp.concatenate(tiles[2:], axis=1)], axis=0
                )
            )
        rows[0, xh, s] = jnp.where(xh == 0, halves[0], halves[1]).astype(jnp.bfloat16)
        half_out[s] = jnp.where(xh == 0, halves[1], halves[0]).astype(jnp.bfloat16)

    @pl.when(answers > 0)
    def _():
        pl.semaphore_wait(ready, answers)

    for s in range(STAGES):
        second_product(s)
        send_rows(s)

    def slot_copy(slot):
        piece = rows.at[slot] if slot else rows.at[0, 0]
        return remote(piece, piece, z_send.at[slot], z_recv.at[slot], here)

    low = lax.broadcasted_iota(jnp.int32, (64, 128), 1) < 64
    sender = xh * 8 + chip

    def mate_gram(b):
        return remote(grams.at[b, 1 - core], mates.at[b], m_send.at[b], m_recv.at[b], mate)

    def gram_copy(b, j):
        slot_u, slot_v = BLOCKS[b]
        to = (plane(OFFSETS[slot_u]) * 2 + core, plane(OFFSETS[slot_v]) * 2 + j)
        own = jnp.logical_and(to[0] == row, to[1] == col)
        return own, remote(sums.at[b, j], parts.at[sender], g_send.at[b], g_recv, to)

    def send_gram(b):
        mate_gram(b).wait_recv()
        sums[b] = grams[b, core] + mates[b]
        for j in range(2):
            own, copy = gram_copy(b, j)

            @pl.when(own)
            def _():
                pltpu.make_async_copy(sums.at[b, j], parts.at[sender], g_recv).start()

            @pl.when(jnp.logical_not(own))
            def _():
                copy.start()

    operands = {}

    def operand(slot):
        if slot not in operands:
            slot_copy(slot).wait_recv()
            whole = rows[slot].reshape(2, STAGES, 2, ROWS, 256)
            flat = jnp.concatenate([whole[:, :, 0].reshape(128, 256), whole[:, :, 1].reshape(128, 256)], axis=1)
            quarters = [flat[32 * i : 32 * i + 32] for i in range(4)]
            operands[slot] = (
                jnp.concatenate([quarters[0], quarters[2]], axis=0),
                jnp.concatenate([quarters[1], quarters[3]], axis=0),
                flat,
                jnp.concatenate([flat[64:], flat[:64]], axis=0),
            )
        return operands[slot]

    def gram_block(b):
        upper, lower, _, _ = operand(BLOCKS[b][0])
        _, _, right, swapped = operand(BLOCKS[b][1])
        m1 = lax.dot_general(upper, right, NT, preferred_element_type=jnp.float32)
        m2 = lax.dot_general(lower, swapped, NT, preferred_element_type=jnp.float32)
        grams[b, :, 0] = jnp.where(low, m1, m2).reshape(2, 32, 128)
        grams[b, :, 1] = jnp.where(low, m2, m1).reshape(2, 32, 128)

    def work_through(groups, eager):
        operands.clear()
        order = [b for group in groups for b in group]
        sent = begun = 0
        for turn, group in enumerate(groups):
            for b in group:
                gram_block(b)
            for b in group:
                mate_gram(b).start()
            ready_to_send = begun + len(group) if turn < eager else begun - BEHIND
            begun += len(group)
            while sent < ready_to_send:
                send_gram(order[sent])
                sent += 1
        for b in order[sent:]:
            send_gram(b)

    first_up = jnp.logical_and(z == 0, xh == 0)
    next_up = jnp.logical_and(z == 1, xh == 0)
    first_down = jnp.logical_and(z < 2, xh == 1)

    @pl.when(first_up)
    def _():
        work_through(GROUPS_UP, 2)

    @pl.when(first_down)
    def _():
        work_through(GROUPS_DOWN, 3)

    @pl.when(next_up)
    def _():
        work_through(GROUPS_NEXT, 4)

    @pl.when(z > 1)
    def _():
        work_through(GROUPS, 2)

    pltpu.make_async_copy(parts, parts, g_recv).wait()
    total = jnp.sum(parts[...], axis=0) * (1.0 / 16384.0)
    first, second = total[:, :64], total[:, 64:]
    out_ref[0:32, :] = jnp.where(core == 0, first, second)
    out_ref[32:64, :] = jnp.where(core == 0, second, first)

    factor_copy.wait_send()
    across_copy.wait_send()
    mate_copy.wait_send()
    for s in range(STAGES):
        stage_copy(s).wait_send()
    for slot in range(len(OFFSETS)):
        slot_copy(slot).wait_send()
    for b in range(len(BLOCKS)):
        mate_gram(b).wait_send()
        for j in range(2):
            own, copy = gram_copy(b, j)

            @pl.when(jnp.logical_not(own))
            def _():
                copy.wait_send()


def on_device(snapshot, basis_two, basis_three):
    anywhere = pl.BlockSpec(memory_space=pl.ANY)
    bf16, f32 = jnp.bfloat16, jnp.float32
    dma = pltpu.SemaphoreType.DMA
    n_blocks = len(BLOCKS)
    return pl.pallas_call(
        kernel,
        out_shape=pltpu.VMEM((64, 64), f32),
        in_specs=[anywhere] * 3,
        out_specs=pl.BlockSpec(memory_space=pltpu.VMEM),
        scratch_shapes=[
            pltpu.VMEM((STAGES, ROWS, 64, 512), bf16),
            pltpu.VMEM((512, 128), bf16),
            pltpu.VMEM((128, 512), bf16),
            pltpu.VMEM((2, 2, 4, 64, 128), bf16),
            pltpu.VMEM((N_COL * 128, 256), bf16),
            pltpu.VMEM((STAGES, N_COL, PAIRS, 16, 128), bf16),
            pltpu.VMEM((STAGES, N_COL, PAIRS, 16, 128), bf16),
            pltpu.VMEM((2, 8 * HALF, 128), f32),
            pltpu.VMEM((STAGES, 2 * ROWS, 256), bf16),
            pltpu.VMEM((4, 2, STAGES, 2 * ROWS, 256), bf16),
            pltpu.VMEM((n_blocks, 2, 2, 32, 128), f32),
            pltpu.VMEM((n_blocks, 2, 32, 128), f32),
            pltpu.VMEM((n_blocks, 2, 32, 128), f32),
            pltpu.VMEM((N_COL, 32, 128), f32),
            dma((STAGES + 2,)),
            dma((6,)),
            dma((STAGES,)),
            dma((STAGES,)),
            dma((4,)),
            dma((4,)),
            dma((n_blocks,)),
            dma((n_blocks,)),
            dma((n_blocks,)),
            dma,
            pltpu.SemaphoreType.REGULAR,
        ],
        compiler_params=pltpu.CompilerParams(
            collective_id=0, has_side_effects=True, vmem_limit_bytes=60 * 1024 * 1024
        ),
    )(snapshot, basis_two, basis_three)


def solution(mesh):
    in_specs = (P("row", "col", None), P("col", None), P())
    return jax.shard_map(
        on_device, mesh=mesh, in_specs=in_specs, out_specs=P("row", "col"), check_vma=False
    )
```

```python
import jax
import jax.numpy as jnp
from jax import lax
from jax.experimental import pallas as pl
from jax.experimental.pallas import tpu as pltpu
from jax.sharding import PartitionSpec as P

MESH = pl.DeviceIdType.MESH
NT = (((1,), (1,)), ((), ()))

N_COL = 16
PLANES = 8
STAGES = 8
BEHIND = 2
GROUPS = ((0,), (1, 2), (5, 3), (6, 7), (4,))
GROUPS_UP = ((0,), (4,), (1, 2), (3, 5), (6, 7))
GROUPS_DOWN = ((0,), (1, 2), (3,), (4, 5), (6, 7))
ROWS = 64 // STAGES
HALF = ROWS // 2
PAIRS = HALF // 2
OFFSETS = (0, -2, -1, 2)
BLOCKS = ((0, 0), (0, 2), (2, 0), (0, 1), (0, 3), (1, 3), (3, 2), (2, 3))


def kernel(
    snap_hbm,
    b2_hbm,
    b3_hbm,
    out_ref,
    snap,
    b3,
    b3t,
    factor,
    weights,
    outgoing,
    incoming,
    pacc,
    half_out,
    rows,
    grams,
    mates,
    sums,
    parts,
    load_sems,
    f_sems,
    a_send,
    a_recv,
    z_send,
    z_recv,
    m_send,
    m_recv,
    g_send,
    g_recv,
    ready,
):
    row = lax.axis_index("row")
    col = lax.axis_index("col")
    z = row // 2
    xh = lax.rem(row, 2)
    core = lax.rem(col, 2)
    chip = col // 2
    x_lo = lax.rem(chip, 2)
    across = (1 - xh, col ^ 2)

    sign = 1 - 2 * xh

    def plane(offset, away=1):
        return lax.rem(z + away * sign * offset + PLANES, PLANES)

    def remote(src, dst, send_sem, recv_sem, device):
        return pltpu.make_async_remote_copy(
            src_ref=src,
            dst_ref=dst,
            send_sem=send_sem,
            recv_sem=recv_sem,
            device_id=device,
            device_id_type=MESH,
        )

    here = (row, col)
    load_b3 = pltpu.make_async_copy(b3_hbm, b3, load_sems.at[STAGES])
    load_b2 = pltpu.make_async_copy(b2_hbm, factor.at[core, x_lo, chip // 2], load_sems.at[STAGES + 1])
    loads = [
        pltpu.make_async_copy(snap_hbm.at[pl.ds(ROWS * s, ROWS)], snap.at[s], load_sems.at[s])
        for s in range(STAGES)
    ]
    load_b3.start()
    loads[0].start()
    load_b2.start()
    for load in loads[1:]:
        load.start()

    barrier = pltpu.get_barrier_semaphore()

    def greet(device):
        pl.semaphore_signal(barrier, inc=1, device_id=device, device_id_type=MESH)

    def greet_column(i, carry):
        greet((row, col ^ i))
        return carry

    lax.fori_loop(1, N_COL, greet_column, 0)
    greet((z * 2 + across[0], across[1]))

    edges = []
    for slot, offset in enumerate(OFFSETS):
        if slot:
            edges.append((plane(offset, -1), plane(offset), (xh, col)))
            edges.append((plane(offset), plane(offset), across))

    def where(test):
        return jnp.where(test, 1, 0)

    greetings, answers = N_COL, 0
    for target, source, (there, at) in edges:

        @pl.when(target > z)
        def _():
            greet((target * 2 + there, at))

        @pl.when(source > z)
        def _():
            greet((source * 2 + there, at))

        greetings = greetings + where(target < z) + where(source < z)
        answers = answers + where(target > z)

    load_b3.wait()
    b3t[...] = b3[...].T

    def first_product(s):
        loads[s].wait()
        left = b3t[...]
        for jp in range(PAIRS):
            j = 2 * jp
            right = jnp.concatenate(
                [snap[s, j], snap[s, HALF + j], snap[s, j + 1], snap[s, HALF + j + 1]], axis=0
            )
            inner = lax.dot_general(left, right, NT, preferred_element_type=jnp.float32)
            pair = jnp.concatenate(
                [inner[:, :128].reshape(N_COL, 8, 128), inner[:, 128:].reshape(N_COL, 8, 128)], axis=1
            ).astype(jnp.bfloat16)
            outgoing[s, :, jp] = pair
        incoming[s, col] = outgoing[s, col ^ (2 * xh)]

    def send_stage(s):
        def body(i, carry):
            peer = col ^ i
            remote(
                outgoing.at[s, peer ^ (2 * xh)], incoming.at[s, col], a_send.at[s], a_recv.at[s], (row, peer)
            ).start()
            return carry

        lax.fori_loop(1, N_COL, body, 0)

    def stage_copy(s):
        most = pl.ds(0, N_COL - 1)
        return remote(outgoing.at[s, most], incoming.at[s, most], a_send.at[s], a_recv.at[s], here)

    first_product(0)
    load_b2.wait()
    pl.semaphore_wait(barrier, greetings)
    for _, source, (there, at) in edges:

        @pl.when(source < z)
        def _():
            pl.semaphore_signal(ready, inc=1, device_id=(source * 2 + there, at), device_id_type=MESH)


    own = factor.at[core, x_lo, chip // 2]
    for y in range(1, 4):
        remote(own, own, f_sems.at[0], f_sems.at[1], (row, col ^ (4 * y))).start()
    send_stage(0)
    for s in range(1, STAGES):
        first_product(s)
        send_stage(s)

    most = factor.at[core, x_lo, pl.ds(0, 3)]
    factor_copy = remote(most, most, f_sems.at[0], f_sems.at[1], here)
    factor_copy.wait_recv()
    line = factor.at[core, x_lo]
    other = factor.at[core, 1 - x_lo]
    across_copy = remote(line, line, f_sems.at[4], f_sems.at[5], (z * 2 + across[0], across[1]))
    across_copy.start()
    remote(other, other, f_sems.at[4], f_sems.at[5], here).wait_recv()
    mate = (row, col ^ 1)
    mine = factor.at[core]
    mate_copy = remote(mine, mine, f_sems.at[2], f_sems.at[3], mate)
    mate_copy.start()
    weights[...] = jnp.zeros_like(weights)
    mate_copy.wait_recv()
    for c in range(N_COL):
        block = factor[c % 2, (c // 2) % 2, c // 4]
        weights[pl.ds(c * 128, 64), :128] = block
        weights[pl.ds(c * 128 + 64, 64), 128:] = block

    def send_rows(s):
        for slot, offset in enumerate(OFFSETS):
            if slot:
                to = (plane(offset, -1) * 2 + xh, col)
                remote(rows.at[0, xh, s], rows.at[slot, xh, s], z_send.at[slot], z_recv.at[slot], to).start()
            to = (plane(offset) * 2 + across[0], across[1])
            remote(half_out.at[s], rows.at[slot, xh, s], z_send.at[slot], z_recv.at[slot], to).start()

    def second_product(s):
        stage_copy(s).wait_recv()
        total = jnp.zeros((8 * HALF, 256), jnp.float32)
        for c in range(0, N_COL, 2):
            left = jnp.concatenate(
                [incoming[s, c].reshape(8 * HALF, 128), incoming[s, c + 1].reshape(8 * HALF, 128)], axis=1
            )
            total = total + jnp.dot(left, weights[pl.ds(c * 128, 256), :], preferred_element_type=jnp.float32)
        pacc[0] = total[:, :128]
        pacc[1] = total[:, 128:]
        halves = []
        for h in range(2):
            tiles = []
            for r in range(4 * h, 4 * h + 4):
                every = pl.ds(r, HALF, stride=8)
                tiles.append(jnp.concatenate([pacc[0, every, :], pacc[1, every, :]], axis=0))
            halves.append(
                jnp.concatenate(
                    [jnp.concatenate(tiles[:2], axis=1), jnp.concatenate(tiles[2:], axis=1)], axis=0
                )
            )
        rows[0, xh, s] = jnp.where(xh == 0, halves[0], halves[1]).astype(jnp.bfloat16)
        half_out[s] = jnp.where(xh == 0, halves[1], halves[0]).astype(jnp.bfloat16)

    @pl.when(answers > 0)
    def _():
        pl.semaphore_wait(ready, answers)

    for s in range(STAGES):
        second_product(s)
        send_rows(s)

    def slot_copy(slot):
        piece = rows.at[slot] if slot else rows.at[0, 0]
        return remote(piece, piece, z_send.at[slot], z_recv.at[slot], here)

    low = lax.broadcasted_iota(jnp.int32, (64, 128), 1) < 64
    sender = xh * 8 + chip

    def mate_gram(b):
        return remote(grams.at[b, 1 - core], mates.at[b], m_send.at[b], m_recv.at[b], mate)

    def gram_copy(b, j):
        slot_u, slot_v = BLOCKS[b]
        to = (plane(OFFSETS[slot_u]) * 2 + core, plane(OFFSETS[slot_v]) * 2 + j)
        own = jnp.logical_and(to[0] == row, to[1] == col)
        return own, remote(sums.at[b, j], parts.at[sender], g_send.at[b], g_recv, to)

    def send_gram(b):
        mate_gram(b).wait_recv()
        sums[b] = grams[b, core] + mates[b]
        for j in range(2):
            own, copy = gram_copy(b, j)

            @pl.when(own)
            def _():
                pltpu.make_async_copy(sums.at[b, j], parts.at[sender], g_recv).start()

            @pl.when(jnp.logical_not(own))
            def _():
                copy.start()

    operands = {}

    def operand(slot):
        if slot not in operands:
            slot_copy(slot).wait_recv()
            whole = rows[slot].reshape(2, STAGES, 2, ROWS, 256)
            flat = jnp.concatenate([whole[:, :, 0].reshape(128, 256), whole[:, :, 1].reshape(128, 256)], axis=1)
            quarters = [flat[32 * i : 32 * i + 32] for i in range(4)]
            operands[slot] = (
                jnp.concatenate([quarters[0], quarters[2]], axis=0),
                jnp.concatenate([quarters[1], quarters[3]], axis=0),
                flat,
                jnp.concatenate([flat[64:], flat[:64]], axis=0),
            )
        return operands[slot]

    def gram_block(b):
        upper, lower, _, _ = operand(BLOCKS[b][0])
        _, _, right, swapped = operand(BLOCKS[b][1])
        m1 = lax.dot_general(upper, right, NT, preferred_element_type=jnp.float32)
        m2 = lax.dot_general(lower, swapped, NT, preferred_element_type=jnp.float32)
        grams[b, :, 0] = jnp.where(low, m1, m2).reshape(2, 32, 128)
        grams[b, :, 1] = jnp.where(low, m2, m1).reshape(2, 32, 128)

    def work_through(groups, eager):
        operands.clear()
        order = [b for group in groups for b in group]
        sent = begun = 0
        for turn, group in enumerate(groups):
            for b in group:
                gram_block(b)
            for b in group:
                mate_gram(b).start()
            ready_to_send = begun + len(group) if turn < eager else begun - BEHIND
            begun += len(group)
            while sent < ready_to_send:
                send_gram(order[sent])
                sent += 1
        for b in order[sent:]:
            send_gram(b)

    first_up = jnp.logical_and(z == 0, xh == 0)
    first_down = jnp.logical_and(z == 0, xh == 1)

    @pl.when(first_up)
    def _():
        work_through(GROUPS_UP, 2)

    @pl.when(first_down)
    def _():
        work_through(GROUPS_DOWN, 3)

    @pl.when(z > 0)
    def _():
        work_through(GROUPS, 2)

    pltpu.make_async_copy(parts, parts, g_recv).wait()
    total = jnp.sum(parts[...], axis=0) * (1.0 / 16384.0)
    first, second = total[:, :64], total[:, 64:]
    out_ref[0:32, :] = jnp.where(core == 0, first, second)
    out_ref[32:64, :] = jnp.where(core == 0, second, first)

    factor_copy.wait_send()
    across_copy.wait_send()
    mate_copy.wait_send()
    for s in range(STAGES):
        stage_copy(s).wait_send()
    for slot in range(len(OFFSETS)):
        slot_copy(slot).wait_send()
    for b in range(len(BLOCKS)):
        mate_gram(b).wait_send()
        for j in range(2):
            own, copy = gram_copy(b, j)

            @pl.when(jnp.logical_not(own))
            def _():
                copy.wait_send()


def on_device(snapshot, basis_two, basis_three):
    anywhere = pl.BlockSpec(memory_space=pl.ANY)
    bf16, f32 = jnp.bfloat16, jnp.float32
    dma = pltpu.SemaphoreType.DMA
    n_blocks = len(BLOCKS)
    return pl.pallas_call(
        kernel,
        out_shape=pltpu.VMEM((64, 64), f32),
        in_specs=[anywhere] * 3,
        out_specs=pl.BlockSpec(memory_space=pltpu.VMEM),
        scratch_shapes=[
            pltpu.VMEM((STAGES, ROWS, 64, 512), bf16),
            pltpu.VMEM((512, 128), bf16),
            pltpu.VMEM((128, 512), bf16),
            pltpu.VMEM((2, 2, 4, 64, 128), bf16),
            pltpu.VMEM((N_COL * 128, 256), bf16),
            pltpu.VMEM((STAGES, N_COL, PAIRS, 16, 128), bf16),
            pltpu.VMEM((STAGES, N_COL, PAIRS, 16, 128), bf16),
            pltpu.VMEM((2, 8 * HALF, 128), f32),
            pltpu.VMEM((STAGES, 2 * ROWS, 256), bf16),
            pltpu.VMEM((4, 2, STAGES, 2 * ROWS, 256), bf16),
            pltpu.VMEM((n_blocks, 2, 2, 32, 128), f32),
            pltpu.VMEM((n_blocks, 2, 32, 128), f32),
            pltpu.VMEM((n_blocks, 2, 32, 128), f32),
            pltpu.VMEM((N_COL, 32, 128), f32),
            dma((STAGES + 2,)),
            dma((6,)),
            dma((STAGES,)),
            dma((STAGES,)),
            dma((4,)),
            dma((4,)),
            dma((n_blocks,)),
            dma((n_blocks,)),
            dma((n_blocks,)),
            dma,
            pltpu.SemaphoreType.REGULAR,
        ],
        compiler_params=pltpu.CompilerParams(
            collective_id=0, has_side_effects=True, vmem_limit_bytes=60 * 1024 * 1024
        ),
    )(snapshot, basis_two, basis_three)


def solution(mesh):
    in_specs = (P("row", "col", None), P("col", None), P())
    return jax.shard_map(
        on_device, mesh=mesh, in_specs=in_specs, out_specs=P("row", "col"), check_vma=False
    )
```
